256 devices in a mesh: graph: 64 (over x, z, core), batch: 4 (over y).
Axes of the slice: x: 4, y: 4, z: 8, core: 2. Of those that a mesh axis runs over, the one named last changes fastest.
Arguments:
- layer_input: bfloat16 [16384, 512], P('graph', 'batch'), may hold values from -6 to 6
- hidden_state: bfloat16 [16384, 512], P('graph', 'batch'), may hold values from -6 to 6
- hidden_grad: bfloat16 [16384, 512], P('graph', 'batch'), may hold values from -6 to 6
- gate_weight: bfloat16 [640, 128], replicated, may hold values from -0.25 to 0.25
- gate_bias: float32 [128], replicated, may hold values from -3 to 3
- candidate_weight: bfloat16 [640, 64], replicated, may hold values from -0.25 to 0.25
- candidate_bias: float32 [64], replicated, may hold values from -3 to 3
- forward_tiles: bfloat16 [128, 3, 128, 128], P('graph'), as said below
- forward_columns: int32 [128, 3], P('graph'), may hold values from 0 to 2
- reverse_tiles: bfloat16 [128, 3, 128, 128], P('graph'), as said below
- reverse_columns: int32 [128, 3], P('graph'), may hold values from 0 to 2
- send_rows: int32 [64, 4, 32], P('graph'), may hold values from 0 to 255
- send_count: int32 [64, 4], P('graph'), may hold values from 1 to 32, as said below
Outputs:
- input_grad: float32 [16384, 512], P('graph', 'batch')
- state_grad: float32 [16384, 512], P('graph', 'batch')
- gate_weight_grad: float32 [640, 128], replicated
- gate_bias_grad: float32 [128], replicated
- candidate_weight_grad: float32 [640, 64], replicated
- candidate_bias_grad: float32 [64], replicated
The draws below stay inside these ranges and needn't reach their ends.
Inputs may be any that keep to these rules, and one draw needn't show every extreme that they name: send_rows[p, j] lists rows of part p that part p + o_j reads; a row may stand in several lists or twice in one. The first send_count[p, j] entries of send_rows[p, j] are live; 32 is reached in every draw. `forward_tiles`: entries are zero or positive. `reverse_tiles`: entries are zero or positive. `forward_columns`: a value below 2 names a block of the part's own rows, a larger one a block of its rim. `reverse_columns`: as for forward_columns.
All inputs are finite; a program needn't handle non-finite values.
Results may differ from the reference program's by a relative error of at most 0.0055.
Values may be sent and summed in bfloat16 or wider, within the bound.
No kernel may reach another device: no remote copies, remote signals or barrier semaphores. Data moves between devices by JAX's collectives and lax.ppermute only.
A program may use at most 64 MiB of HBM per device.

```python
import math
import jax
import jax.numpy as jnp
from jax import lax

HID = 64
INP = 64
KS = 5
TILE = 128
TPR = 3
REACH = 2
SLOT = 32
NODE_DEV = 256
NB = 2
HALO = 128
NCB = 3
PARTS_SIZE = 64
NODES = 16384
BATCH = 8
CH = 128


mean_degree = 8.0


def tile_values(key):
    mask_key, value_key = jax.random.split(key)
    shape = (NODES // TILE, TPR, TILE, TILE)
    chance = mean_degree / (TPR * TILE)
    present = jax.random.uniform(mask_key, shape, dtype=jnp.float32) < chance
    magnitude = jax.random.uniform(value_key, shape, dtype=jnp.float32, minval=0.05, maxval=0.2)
    return jnp.where(present, magnitude, 0.0).astype(jnp.bfloat16)


def draw_forward_tiles(key, part):
    return tile_values(jax.random.fold_in(key, 11))


def draw_reverse_tiles(key, part):
    return tile_values(jax.random.fold_in(key, 12))


def draw_send_count(key, part):
    count_key, spot_key = jax.random.split(jax.random.fold_in(key, 13))
    entries = PARTS_SIZE * 2 * REACH
    counts = jax.random.randint(count_key, (entries,), 1, SLOT + 1)
    spot = jax.random.randint(spot_key, (), 0, entries)
    filled = jnp.where(jnp.arange(entries) == spot, SLOT, counts)
    return filled.reshape(PARTS_SIZE, 2 * REACH).astype(jnp.int32)


def plant(values, rng, least, top_value):
    spot = [jax.random.randint(jax.random.fold_in(rng, axis), (), 0, length) for axis, length in enumerate(values.shape)]
    widest = values.shape.index(max(values.shape))
    beside = spot[:widest] + [(spot[widest] + 1) % values.shape[widest]] + spot[widest + 1:]
    return values.at[tuple(spot)].set(least).at[tuple(beside)].set(top_value)


def block_levels(rng, dims, cuts, least, largest):
    def one(dim, parts):
        draws = jax.random.uniform(jax.random.fold_in(jax.random.fold_in(rng, 6), dim), (parts,), jnp.float32, least / len(cuts), largest / len(cuts))
        return jnp.repeat(jnp.exp(draws), dims[dim] // parts).reshape((-1,) + (1,) * (len(dims) - dim - 1))

    loudness = one(*cuts[0])
    for cut in cuts[1:]:
        loudness = loudness * one(*cut)
    return loudness


def centred(key, shape, scale, bound, cuts=(), kind=jnp.bfloat16):
    values = scale * jax.random.normal(key, shape, jnp.float32)
    if cuts:
        values = values * block_levels(key, shape, cuts, -0.22, 0.18)
    return jnp.clip(values, -bound, bound).astype(kind)


def setup_inputs(seed: int = 0) -> dict:
    seeds = jax.random.split(jax.random.key(seed), 14)
    return {
        "layer_input": centred(seeds[0], (NODES, BATCH * INP), 1.0, 6.0, ((0, 64), (1, 4))),
        "hidden_state": centred(seeds[1], (NODES, BATCH * HID), 1.0, 6.0, ((0, 64), (1, 4))),
        "hidden_grad": centred(seeds[2], (NODES, BATCH * HID), 1.0, 6.0, ((0, 64), (1, 4))),
        "gate_weight": centred(seeds[3], (KS * CH, 2 * HID), (KS * CH) ** -0.5, 0.25),
        "gate_bias": centred(seeds[4], (2 * HID,), 0.5, 3.0, (), jnp.float32),
        "candidate_weight": centred(seeds[5], (KS * CH, HID), (KS * CH) ** -0.5, 0.25),
        "candidate_bias": centred(seeds[6], (HID,), 0.5, 3.0, (), jnp.float32),
        "forward_tiles": draw_forward_tiles(jax.random.fold_in(seeds[13], 71), 0),
        "forward_columns": plant(jax.random.randint(seeds[8], (NODES // TILE, TPR), 0, NCB), jax.random.fold_in(seeds[8], 1), 0, NCB - 1).astype(jnp.int32),
        "reverse_tiles": draw_reverse_tiles(jax.random.fold_in(seeds[13], 71), 0),
        "reverse_columns": plant(jax.random.randint(seeds[10], (NODES // TILE, TPR), 0, NCB), jax.random.fold_in(seeds[10], 1), 0, NCB - 1).astype(jnp.int32),
        "send_rows": plant(jax.random.randint(seeds[11], (PARTS_SIZE, 2 * REACH, SLOT), 0, NODE_DEV), jax.random.fold_in(seeds[11], 1), 0, NODE_DEV - 1).astype(jnp.int32),
        "send_count": draw_send_count(jax.random.fold_in(seeds[13], 71), 0),
    }


def rim_sources(send_rows, send_count):
    part_ids = jnp.arange(PARTS_SIZE, dtype=jnp.int32)
    offsets = jnp.array([(number // 2 + 1) * (1 - 2 * (number % 2)) for number in range(2 * REACH)], dtype=jnp.int32)
    source = part_ids[:, None] - offsets[None, :]
    inside = (source >= 0) & (source < PARTS_SIZE)
    clipped = jnp.clip(source, 0, PARTS_SIZE - 1).astype(jnp.int32)
    rim_sets = jnp.arange(2 * REACH, dtype=jnp.int32)
    listed = send_rows[clipped, rim_sets[None, :]]
    counts = send_count[clipped, rim_sets[None, :]]
    slot_ids = jnp.arange(SLOT, dtype=jnp.int32)
    valid_mask = inside[:, :, None] & (slot_ids[None, None, :] < counts[:, :, None])
    global_rows = (clipped[:, :, None] * NODE_DEV + listed).astype(jnp.int32)
    return (global_rows.reshape(PARTS_SIZE, HALO), valid_mask.reshape(PARTS_SIZE, HALO))

def spread(values, tiles, columns, sources):
    global_rows, valid_mask = sources
    feature_width = values.shape[1]

    def per_part(part_id):
        local_part = lax.dynamic_slice_in_dim(values, part_id * NODE_DEV, NODE_DEV, 0)
        rim_rows = jnp.where(valid_mask[part_id][:, None], values[global_rows[part_id]], jnp.zeros((), values.dtype))
        blocks = jnp.concatenate([local_part, rim_rows], 0).reshape(NCB, TILE, feature_width)
        own_tiles = lax.dynamic_slice_in_dim(tiles, part_id * NB, NB, 0)
        own_columns = lax.dynamic_slice_in_dim(columns, part_id * NB, NB, 0)
        picked = jnp.take(blocks, own_columns, axis=0)
        result = jnp.einsum('itac,itcm->iam', own_tiles.astype(jnp.float32), picked.astype(jnp.float32))
        return result.reshape(NODE_DEV, feature_width)
    return lax.map(per_part, jnp.arange(PARTS_SIZE, dtype=jnp.int32)).reshape(NODES, feature_width)

def gather_back(cotangents, tiles, columns, sources):
    global_rows, valid_mask = sources
    feature_width = cotangents.shape[1]

    def per_part(part_id):
        row_blocks = lax.dynamic_slice_in_dim(cotangents, part_id * NODE_DEV, NODE_DEV, 0).reshape(NB, TILE, feature_width)
        own_tiles = lax.dynamic_slice_in_dim(tiles, part_id * NB, NB, 0)
        own_columns = lax.dynamic_slice_in_dim(columns, part_id * NB, NB, 0)
        products = jnp.einsum('itac,iam->itcm', own_tiles.astype(jnp.float32), row_blocks.astype(jnp.float32))
        select = (own_columns[:, :, None] == jnp.arange(NCB, dtype=jnp.int32)[None, None, :]).astype(jnp.float32)
        blocks = jnp.einsum('itb,itcm->bcm', select, products, precision=lax.Precision.HIGHEST)
        blocks = blocks.reshape(NCB * TILE, feature_width)
        return (blocks[:NODE_DEV], blocks[NODE_DEV:])
    local_part, rim_rows = lax.map(per_part, jnp.arange(PARTS_SIZE, dtype=jnp.int32))
    rim_rows = rim_rows.reshape(PARTS_SIZE * HALO, feature_width)
    rim_rows = jnp.where(valid_mask.reshape(-1)[:, None], rim_rows, jnp.zeros((), rim_rows.dtype))
    return local_part.reshape(NODES, feature_width).at[global_rows.reshape(-1)].add(rim_rows)

def supports(values, graph_links, sources):
    forward_tiles, forward_columns, reverse_tiles, reverse_columns = graph_links
    base_field = values.astype(jnp.float32)
    first_forward = spread(values, forward_tiles, forward_columns, sources).astype(jnp.bfloat16)
    second_forward = (2.0 * spread(first_forward, forward_tiles, forward_columns, sources) - base_field).astype(jnp.bfloat16)
    first_reverse = spread(values, reverse_tiles, reverse_columns, sources).astype(jnp.bfloat16)
    second_reverse = (2.0 * spread(first_reverse, reverse_tiles, reverse_columns, sources) - base_field).astype(jnp.bfloat16)
    members = [values, first_forward, second_forward, first_reverse, second_reverse]
    return jnp.concatenate([member.reshape(-1, CH) for member in members], 1)

def back_supports(flat_grads, graph_links, sources):
    forward_tiles, forward_columns, reverse_tiles, reverse_columns = graph_links
    per_node = flat_grads.reshape(NODES, BATCH, KS, CH)
    members = [per_node[:, :, support].reshape(NODES, BATCH * CH) for support in range(KS)]
    first_forward = members[1] + 2.0 * gather_back(members[2].astype(jnp.bfloat16), forward_tiles, forward_columns, sources)
    first_reverse = members[3] + 2.0 * gather_back(members[4].astype(jnp.bfloat16), reverse_tiles, reverse_columns, sources)
    summed = members[0] - members[2] - members[4]
    summed = summed + gather_back(first_forward.astype(jnp.bfloat16), forward_tiles, forward_columns, sources)
    summed = summed + gather_back(first_reverse.astype(jnp.bfloat16), reverse_tiles, reverse_columns, sources)
    return summed.reshape(NODES * BATCH, CH)

def reference(layer_input, hidden_state, hidden_grad, gate_weight, gate_bias, candidate_weight, candidate_bias, forward_tiles, forward_columns, reverse_tiles, reverse_columns, send_rows, send_count):
    sources = rim_sources(send_rows, send_count)
    graph_links = (forward_tiles, forward_columns, reverse_tiles, reverse_columns)
    input_field = layer_input.reshape(NODES, BATCH, INP)
    hidden_field = hidden_state.reshape(NODES, BATCH, HID)
    stacked = jnp.concatenate([input_field, hidden_field], 2).reshape(NODES, BATCH * CH)
    gate_rows = supports(stacked, graph_links, sources)
    gate_values = jax.nn.sigmoid(jnp.dot(gate_rows, gate_weight, preferred_element_type=jnp.float32) + gate_bias)
    reset_gate = gate_values[:, :HID]
    update = gate_values[:, HID:]
    hidden_rows = hidden_state.reshape(-1, HID).astype(jnp.float32)
    gated = (reset_gate * hidden_rows).astype(jnp.bfloat16)
    candidate_input = jnp.concatenate([input_field, gated.reshape(NODES, BATCH, HID)], 2).reshape(NODES, BATCH * CH)
    candidate_rows = supports(candidate_input, graph_links, sources)
    candidate = jnp.tanh(jnp.dot(candidate_rows, candidate_weight, preferred_element_type=jnp.float32) + candidate_bias)
    cotangent = hidden_grad.reshape(-1, HID).astype(jnp.float32)
    update_grad = cotangent * (hidden_rows - candidate)
    candidate_grad = (cotangent * (1.0 - update) * (1.0 - candidate * candidate)).astype(jnp.bfloat16)
    norm_scale = 1.0 / math.sqrt(NODES * BATCH)
    candidate_sums = jnp.dot(candidate_rows.T, candidate_grad, preferred_element_type=jnp.float32) * norm_scale
    candidate_totals = lax.optimization_barrier(jnp.sum(candidate_grad.astype(jnp.float32), 0)) * norm_scale
    mixed_grad = back_supports(jnp.dot(candidate_grad, candidate_weight.T, preferred_element_type=jnp.float32), graph_links, sources)
    gated_grad = mixed_grad[:, INP:]
    reset_grad = gated_grad * hidden_rows
    gate_grad = jnp.concatenate([reset_grad * reset_gate * (1.0 - reset_gate), update_grad * update * (1.0 - update)], 1).astype(jnp.bfloat16)
    gate_sums = jnp.dot(gate_rows.T, gate_grad, preferred_element_type=jnp.float32) * norm_scale
    gate_totals = lax.optimization_barrier(jnp.sum(gate_grad.astype(jnp.float32), 0)) * norm_scale
    stacked_grad = back_supports(jnp.dot(gate_grad, gate_weight.T, preferred_element_type=jnp.float32), graph_links, sources)
    input_total = mixed_grad[:, :INP] + stacked_grad[:, :INP]
    hidden_total = cotangent * update + gated_grad * reset_gate + stacked_grad[:, INP:]
    return (input_total.reshape(NODES, BATCH * INP), hidden_total.reshape(NODES, BATCH * HID), gate_sums, gate_totals, candidate_sums, candidate_totals)
```

```python
import math

import jax
import jax.numpy as jnp
from jax import lax
from jax.experimental import pallas as pl
from jax.experimental.pallas import tpu as pltpu
from jax.sharding import PartitionSpec as P

HID = 64
KS = 5
CH = 128
PART = 256
PAIR = 2 * PART
HALO = 128
SLOT = 32
EXT = PART + HALO
WIDE = KS * CH + 128
BF = jnp.bfloat16
F32 = jnp.float32


def core_id():
    return lax.rem(lax.axis_index("graph"), 2)


def chip_id():
    return lax.div(lax.axis_index("graph"), 2)


def call(body, outs, args, name, flops=1 << 20, scratch=()):
    whole = pl.BlockSpec(memory_space=pltpu.VMEM)
    return pl.pallas_call(
        body,
        out_shape=[jax.ShapeDtypeStruct(shape, dtype) for shape, dtype in outs],
        in_specs=[whole] * len(args),
        out_specs=[whole] * len(outs),
        scratch_shapes=list(scratch),
        compiler_params=pltpu.CompilerParams(vmem_limit_bytes=24 << 20),
        cost_estimate=pl.CostEstimate(flops=flops, bytes_accessed=1 << 20, transcendentals=0),
        name=name,
    )(*args)


def mm(left, right):
    return jnp.dot(left, right, preferred_element_type=F32)


def mm_t(left, right):
    return lax.dot_general(left, right, (((1,), (1,)), ((), ())), preferred_element_type=F32)


def t_mm(left, right):
    return lax.dot_general(left, right, (((0,), (0,)), ((), ())), preferred_element_type=F32)


def rows_at(index, size):
    return pl.ds(pl.multiple_of(index * size, size), size)


def from_ends(before, after, count):
    chip = chip_id()
    before = jnp.where(chip > 0, before, jnp.zeros_like(before))
    after = jnp.where(chip < count - 1, after, jnp.zeros_like(after))
    return before, after


def send_lists(picks, values, later, earlier, inner):
    out_a = mm(picks[:HALO], values[:PART]).astype(BF)
    out_b = mm(picks[HALO:], values[PART:]).astype(BF)
    later[...] = jnp.concatenate([out_a[64:96], out_b[0:32], out_b[64:96]], 0)
    earlier[...] = jnp.concatenate([out_a[32:64], out_a[96:128], out_b[96:128]], 0)
    inner[...] = jnp.concatenate([out_b[32:64], out_a[0:32]], 0)


def rims(before, after, inner, count):
    before, after = from_ends(before[...], after[...], count)
    inner = inner[...]
    rim_a = jnp.concatenate([before[32:64], inner[0:32], before[0:32], after[32:64]], 0)
    rim_b = jnp.concatenate([inner[32:64], after[0:32], before[64:96], after[64:96]], 0)
    return rim_a, rim_b


def return_lists(rim_a, rim_b, later, earlier, inner):
    rim_a = rim_a.astype(BF)
    rim_b = rim_b.astype(BF)
    earlier[...] = jnp.concatenate([rim_a[64:96], rim_a[0:32], rim_b[64:96]], 0)
    later[...] = jnp.concatenate([rim_b[32:64], rim_a[96:128], rim_b[96:128]], 0)
    inner[...] = jnp.concatenate([rim_a[32:64], rim_b[0:32]], 0)


def arrivals(before, after, inner, count):
    before, after = from_ends(before[...], after[...], count)
    inner = inner[...]
    to_a = jnp.concatenate([inner[32:64], before[0:32], after[0:32], before[32:64]], 0)
    to_b = jnp.concatenate([after[32:64], inner[0:32], after[64:96], before[64:96]], 0)
    return to_a, to_b


def pack_kernel(x_ref, h_ref, c_ref, meta_ref, out_ref):
    first = core_id() == 0
    for place, ref in enumerate((x_ref, h_ref, c_ref)):
        value = ref[...]
        out_ref[:, place * HID : (place + 1) * HID] = jnp.where(
            first, value[:, HID:], value[:, :HID]
        )
    out_ref[:, 3 * HID :] = meta_ref[...]


def picks_of(row_column):
    lanes = lax.broadcasted_iota(jnp.int32, (HALO, PART), 1)
    return jnp.where(lanes == row_column.astype(F32).astype(jnp.int32), 1.0, 0.0).astype(BF)


def start_kernel(
    x_ref, h_ref, c_ref, meta_ref, got_ref, v_ref, cot_ref, pick_ref, later, earlier, inner
):
    core = core_id()
    first = core == 0
    own = []
    for ref in (x_ref, h_ref, c_ref):
        value = ref[...]
        own.append(jnp.where(first, value[:, :HID], value[:, HID:]))
    here = rows_at(core, PART)
    there = rows_at(1 - core, PART)
    v_ref[here, :] = jnp.concatenate(own[:2], 1)
    v_ref[there, :] = got_ref[:, : 2 * HID]
    cot_ref[here, :] = own[2]
    cot_ref[there, :] = got_ref[:, 2 * HID : 3 * HID]
    pick_ref[rows_at(core, HALO), :] = picks_of(meta_ref[:HALO, 0:1])
    pick_ref[rows_at(1 - core, HALO), :] = picks_of(got_ref[:HALO, 3 * HID : 3 * HID + 1])
    send_lists(pick_ref[...], v_ref[...], later, earlier, inner)


def map_kernel(f_ref, r_ref, f_got, r_got, meta_ref, got_ref, map_ref, turned_ref):
    core = core_id()
    own_columns = meta_ref[:HALO, :].astype(F32)
    got_columns = got_ref[:HALO, 3 * HID :].astype(F32)
    for slot, pair, columns in (
        (core, (f_ref, r_ref), own_columns),
        (1 - core, (f_got, r_got), got_columns),
    ):
        map_part = map_ref.at[rows_at(slot, 2 * PART), :]
        turned_part = turned_ref.at[rows_at(slot, EXT), :]
        for way, tiles in enumerate(pair):
            for row in range(2):
                where_to = [columns[:, 1 + way * 6 + row * 3 + t :][:, :1] for t in range(3)]
                values = [tiles[row, t].astype(F32) for t in range(3)]
                at = way * PART + row * 128
                for block in range(3):
                    total = jnp.zeros((128, 128), F32)
                    for t in range(3):
                        total = total + jnp.where(where_to[t] == block, values[t], 0.0)
                    map_part[at : at + 128, block * 128 : block * 128 + 128] = total.astype(BF)
                    turned_part[block * 128 : block * 128 + 128, at : at + 128] = total.T.astype(BF)


def gate_hop_kernel(
    count, v_ref, map_ref, pick_ref, before, after, inner, hop_ref, later, earlier, inner_out
):
    rim_a, rim_b = rims(before, after, inner, count)
    for part, rim in enumerate((rim_a, rim_b)):
        at = slice(part * PART, (part + 1) * PART)
        full = jnp.concatenate([v_ref[at, :], rim], 0)
        both = mm(map_ref[part * PAIR : (part + 1) * PAIR, :], full).astype(BF)
        hop_ref[at, :] = jnp.concatenate([both[:PART], both[PART:]], 1)
    send_lists(pick_ref[...], hop_ref[...], later, earlier, inner_out)


def gate_kernel(
    count, v_ref, hop_ref, map_ref, pick_ref, before, after, inner, weight_ref, bias_ref,
    rows_ref, gates_ref, gated_ref, later, earlier, inner_out,
):
    rim_a, rim_b = rims(before, after, inner, count)
    rows_ref[:, 0:CH] = v_ref[...]
    rows_ref[:, CH : 2 * CH] = hop_ref[:, :CH]
    rows_ref[:, 3 * CH : 4 * CH] = hop_ref[:, CH:]
    rows_ref[:, KS * CH :] = jnp.ones((PAIR, 128), BF)
    for part, rim in enumerate((rim_a, rim_b)):
        at = slice(part * PART, (part + 1) * PART)
        base = v_ref[at, :].astype(F32)
        full = jnp.concatenate([hop_ref[at, :], rim], 0)
        for way in range(2):
            operator = map_ref[part * PAIR + way * PART : part * PAIR + (way + 1) * PART, :]
            second = 2.0 * mm(operator, full[:, way * CH : (way + 1) * CH]) - base
            place = (2 + 2 * way) * CH
            rows_ref[at, place : place + CH] = second.astype(BF)
    gates = jax.nn.sigmoid(mm(rows_ref[:, : KS * CH], weight_ref[...]) + bias_ref[...])
    gates_ref[...] = gates
    gated = (gates[:, :HID] * v_ref[:, HID:].astype(F32)).astype(BF)
    gated_ref[...] = gated
    send_lists(pick_ref[...], gated, later, earlier, inner_out)


def candidate_hop_kernel(
    count, gated_ref, map_ref, pick_ref, before, after, inner, hop_ref, later, earlier, inner_out
):
    rim_a, rim_b = rims(before, after, inner, count)
    for part, rim in enumerate((rim_a, rim_b)):
        at = slice(part * PART, (part + 1) * PART)
        full = jnp.concatenate([gated_ref[at, :], rim], 0)
        both = mm(map_ref[part * PAIR : (part + 1) * PAIR, :], full)
        hop_ref[at, :] = jnp.concatenate([both[:PART], both[PART:]], 1).astype(BF)
    send_lists(pick_ref[...], hop_ref[...], later, earlier, inner_out)


def candidate_kernel(
    count, rows_ref, gated_ref, hop_ref, map_ref, turned_ref, before, after, inner, gates_ref,
    cot_ref, weight_ref, bias_ref, mixed_rows_ref, grads_ref, later, earlier, inner_out,
):
    rim_a, rim_b = rims(before, after, inner, count)
    gated = gated_ref[...]
    base = gated.astype(F32)
    seconds = [[], []]
    for part, rim in enumerate((rim_a, rim_b)):
        at = slice(part * PART, (part + 1) * PART)
        full = jnp.concatenate([hop_ref[at, :], rim], 0)
        for way in range(2):
            operator = map_ref[part * PAIR + way * PART : part * PAIR + (way + 1) * PART, :]
            second = 2.0 * mm(operator, full[:, way * HID : (way + 1) * HID]) - base[at]
            seconds[way].append(second.astype(BF))
    hop = hop_ref[...]
    members = [
        gated,
        hop[:, :HID],
        jnp.concatenate(seconds[0], 0),
        hop[:, HID:],
        jnp.concatenate(seconds[1], 0),
    ]
    for k, member in enumerate(members):
        mixed_rows_ref[:, k * CH : (k + 1) * CH] = jnp.concatenate(
            [rows_ref[:, k * CH : k * CH + HID], member], 1
        )
    mixed_rows_ref[:, KS * CH :] = jnp.ones((PAIR, 128), BF)
    candidate = jnp.tanh(mm(mixed_rows_ref[:, : KS * CH], weight_ref[...]) + bias_ref[...])
    hidden = rows_ref[:, HID:CH].astype(F32)
    cotangent = cot_ref[...].astype(F32)
    update = gates_ref[:, HID:]
    update_grad = cotangent * (hidden - candidate)
    grad = (cotangent * (1.0 - update) * (1.0 - candidate * candidate)).astype(BF)
    grads_ref[...] = jnp.concatenate(
        [grad, (update_grad * update * (1.0 - update)).astype(BF)], 1
    )
    back = []
    for part in range(2):
        turned = turned_ref[part * EXT + PART : (part + 1) * EXT, :]
        mine = grad[part * PART : (part + 1) * PART]
        back.append(
            jnp.concatenate([mm(turned[:, :PART], mine), mm(turned[:, PART:], mine)], 1)
        )
    return_lists(back[0], back[1], later, earlier, inner_out)


def candidate_sums_kernel(rows_ref, mixed_rows_ref, grads_ref, sums_ref):
    sums_ref[:HID, :] = t_mm(grads_ref[:, :HID], mixed_rows_ref[...])
    sums_ref[HID:, :] = t_mm(grads_ref[:, HID:], rows_ref[...])


def back_hop(grad, width, turned_ref, pick_ref, to_a, to_b, weight_ref, later, earlier, inner_out, base_ref):
    columns = weight_ref.shape[1]
    arrived = []
    firsts = []
    for part, coming in enumerate((to_a, to_b)):
        turned = turned_ref[part * EXT : part * EXT + PART, :]
        mine = grad[part * PART : (part + 1) * PART]
        back = t_mm(pick_ref[part * HALO : (part + 1) * HALO, :], coming)
        pair = []
        for way in range(2):
            once = mm(turned[:, way * PART : (way + 1) * PART], mine)
            once = (2.0 * (once + back[:, way * width : (way + 1) * width])).astype(BF)
            first = weight_ref[(1 + 2 * way) * CH : (2 + 2 * way) * CH, :]
            second = weight_ref[(2 + 2 * way) * CH : (3 + 2 * way) * CH, :]
            pair.append((mm_t(mine, first) + mm_t(once, second)).astype(BF))
        firsts.append(jnp.concatenate(pair, 0))
    rim = []
    for part in range(2):
        mine = grad[part * PART : (part + 1) * PART]
        product = mm(turned_ref[part * EXT : (part + 1) * EXT, :], firsts[part])
        rim.append(product[PART:])
        base_ref[part * PART : (part + 1) * PART, :] = (
            product[:PART]
            + mm_t(mine, weight_ref[0:CH, :])
            - mm_t(mine, weight_ref[2 * CH : 3 * CH, :])
            - mm_t(mine, weight_ref[4 * CH : 5 * CH, :])
        )
    return_lists(rim[0], rim[1], later, earlier, inner_out)


def candidate_back_kernel(
    count, grads_ref, turned_ref, pick_ref, before, after, inner, weight_ref,
    base_ref, later, earlier, inner_out,
):
    to_a, to_b = arrivals(before, after, inner, count)
    back_hop(
        grads_ref[:, :HID], HID, turned_ref, pick_ref, to_a, to_b, weight_ref,
        later, earlier, inner_out, base_ref,
    )


def mixed_kernel(
    count, base_ref, before, after, inner, pick_ref, turned_ref, gates_ref, rows_ref, grads_ref,
    mixed_ref, gate_grads_ref, later, earlier, inner_out,
):
    to_a, to_b = arrivals(before, after, inner, count)
    for part, coming in enumerate((to_a, to_b)):
        at = slice(part * PART, (part + 1) * PART)
        mixed_ref[at, :] = base_ref[at, :] + t_mm(
            pick_ref[part * HALO : (part + 1) * HALO, :], coming
        )
    reset = gates_ref[:, :HID]
    hidden = rows_ref[:, HID:CH].astype(F32)
    grad = mixed_ref[:, HID:] * hidden * reset * (1.0 - reset)
    gate_grads_ref[...] = jnp.concatenate([grad.astype(BF), grads_ref[:, HID:]], 1)
    back = []
    for part in range(2):
        turned = turned_ref[part * EXT + PART : (part + 1) * EXT, :]
        mine = gate_grads_ref[part * PART : (part + 1) * PART, :]
        back.append(
            jnp.concatenate([mm(turned[:, :PART], mine), mm(turned[:, PART:], mine)], 1)
        )
    return_lists(back[0], back[1], later, earlier, inner_out)


def sums_kernel(rows_ref, gate_grads_ref, early_ref, keep_ref, send_ref, all_ref):
    half = 3 * HID // 2
    core = core_id()
    all_ref[:HID, :] = early_ref[:HID, :]
    all_ref[HID : 2 * HID, :] = t_mm(gate_grads_ref[:, :HID], rows_ref[...])
    all_ref[2 * HID :, :] = early_ref[HID:, :]
    keep_ref[...] = all_ref[rows_at(core, half), :]
    send_ref[...] = all_ref[rows_at(1 - core, half), :].astype(BF)


def gate_back_kernel(
    count, gate_grads_ref, turned_ref, pick_ref, before, after, inner, weight_ref,
    base_ref, later, earlier, inner_out,
):
    to_a, to_b = arrivals(before, after, inner, count)
    back_hop(
        gate_grads_ref[...], CH, turned_ref, pick_ref, to_a, to_b, weight_ref,
        later, earlier, inner_out, base_ref,
    )


def last_kernel(
    count, base_ref, before, after, inner, pick_ref, mixed_ref, gates_ref, cot_ref,
    keep_ref, send_ref, all_ref,
):
    core = core_id()
    to_a, to_b = arrivals(before, after, inner, count)
    cotangent = cot_ref[...].astype(F32)
    mixed = mixed_ref[...]
    gates = gates_ref[...]
    direct = jnp.concatenate(
        [mixed[:, :HID], cotangent * gates[:, HID:] + mixed[:, HID:] * gates[:, :HID]], 1
    )
    for part, coming in enumerate((to_a, to_b)):
        at = slice(part * PART, (part + 1) * PART)
        all_ref[at, :] = (
            base_ref[at, :]
            + t_mm(pick_ref[part * HALO : (part + 1) * HALO, :], coming)
            + direct[at]
        )
    keep_ref[...] = all_ref[rows_at(core, PART), :]
    send_ref[...] = all_ref[rows_at(1 - core, PART), :]


def place_kernel(keep_ref, got_ref, input_ref, state_ref):
    first = core_id() == 0
    keep = keep_ref[...]
    got = got_ref[...]
    low = jnp.where(first, keep, got)
    high = jnp.where(first, got, keep)
    input_ref[...] = jnp.concatenate([low[:, :HID], high[:, :HID]], 1)
    state_ref[...] = jnp.concatenate([low[:, HID:], high[:, HID:]], 1)


def turned_by(value, axis, steps):
    count = lax.axis_size(axis)
    return lax.ppermute(value, axis, [(i, (i + steps) % count) for i in range(count)])


def swapped(value):
    count = lax.axis_size("graph")
    return lax.ppermute(value, "graph", [(i, i ^ 1) for i in range(count)])


def in_rings(value, stride, length, steps):
    count = lax.axis_size("graph")
    pairs = []
    for i in range(count):
        chip, core = divmod(i, 2)
        high, rest = divmod(chip, stride * length)
        place, low = divmod(rest, stride)
        place = (place + steps) % length
        pairs.append((i, 2 * (high * stride * length + place * stride + low) + core))
    return lax.ppermute(value, "graph", pairs)


def exchange(later, earlier):
    return turned_by(later, "graph", 2), turned_by(earlier, "graph", -2)


def split_kernel(quarters, size, keep_ref, got_ref, *rest):
    outs, all_ref = rest[:-1], rest[-1]
    me = lax.axis_index("batch")
    all_ref[...] = keep_ref[...] + got_ref[...].astype(F32)
    outs[0][...] = all_ref[rows_at(me, size), :]
    for step in range(1, quarters):
        target = lax.rem(me + step, quarters)
        outs[step][...] = all_ref[rows_at(target, size), :].astype(BF)


def joined_kernel(own_ref, *rest):
    total = own_ref[...].astype(F32)
    for ref in rest[:-1]:
        total = total + ref[...].astype(F32)
    rest[-1][...] = total.astype(BF)


def ring_total_kernel(*refs):
    values = [ref[...].astype(F32) for ref in refs[:-1]]
    while len(values) > 1:
        half = len(values) // 2
        values = [values[i] + values[i + half] for i in range(half)]
    refs[-1][...] = values[0].astype(BF)


def gathered_kernel(quarters, size, *refs):
    me = lax.axis_index("batch")
    for step in range(quarters):
        source = lax.rem(me - step + quarters, quarters)
        refs[-1][rows_at(source, size), :] = refs[step][...]


def scaled_kernel(scale, mine_ref, got_ref, gate_ref, gate_bias_ref, candidate_ref, candidate_bias_ref, all_ref):
    half = 3 * HID // 2
    core = core_id()
    all_ref[rows_at(core, half), :] = mine_ref[...].astype(F32) * scale
    all_ref[rows_at(1 - core, half), :] = got_ref[...].astype(F32) * scale
    for k in range(KS):
        at = slice(k * CH, (k + 1) * CH)
        candidate_ref[at, :] = all_ref[:HID, at].T
        gate_ref[at, :] = all_ref[HID:, at].T
    candidate_bias_ref[...] = all_ref[:HID, KS * CH :].T[:8]
    gate_bias_ref[...] = all_ref[HID:, KS * CH :].T[:8]


def ring_total(value, stride, length, axis=None):
    shape = value.shape
    values = [value]
    for step in range(1, length):
        values.append(in_rings(value, stride, length, step))
    return call(ring_total_kernel, [(shape, BF)], values, "ring_total")[0]


def total_over_all(keep, send, scale):
    quarters = lax.axis_size("batch")
    chips = lax.axis_size("graph") // 2
    half = 3 * HID // 2
    size = half // quarters
    piece = (size, WIDE)
    got = swapped(send)
    pieces = call(
        lambda *refs: split_kernel(quarters, size, *refs),
        [(piece, F32)] + [(piece, BF)] * (quarters - 1),
        [keep, got],
        "split",
        scratch=[pltpu.VMEM((half, WIDE), F32)],
    )
    arrived = [turned_by(pieces[step], "batch", step) for step in range(1, quarters)]
    mine = call(joined_kernel, [(piece, BF)], [pieces[0]] + arrived, "joined")[0]
    stride = 1
    for length in ring_lengths(chips):
        mine = ring_total(mine, stride, length)
        stride *= length
    around = [mine] + [turned_by(mine, "batch", step) for step in range(1, quarters)]
    mine = call(
        lambda *refs: gathered_kernel(quarters, size, *refs),
        [((half, WIDE), BF)],
        around,
        "gathered",
    )[0]
    got = swapped(mine)
    return call(
        lambda *refs: scaled_kernel(scale, *refs),
        [((KS * CH, CH), F32), ((8, CH), F32), ((KS * CH, HID), F32), ((8, HID), F32)],
        [mine, got],
        "scaled",
        scratch=[pltpu.VMEM((2 * half, WIDE), F32)],
    )


def ring_lengths(chips):
    lengths = []
    if chips % 8 == 0:
        lengths = [2, 4]
        chips //= 8
    while chips > 1:
        length = 4 if chips % 4 == 0 else 2
        lengths.append(length)
        chips //= length
    return lengths


def on_device(
    layer_input,
    hidden_state,
    hidden_grad,
    gate_weight,
    gate_bias,
    candidate_weight,
    candidate_bias,
    forward_tiles,
    forward_columns,
    reverse_tiles,
    reverse_columns,
    send_rows,
    send_count,
):
    count = lax.axis_size("graph") // 2

    def with_count(body):
        return lambda *refs: body(count, *refs)

    slots = jnp.arange(SLOT, dtype=jnp.int32)
    listed = jnp.where(slots[None, :] < send_count[0][:, None], send_rows[0], -1).reshape(HALO)
    listed = jnp.pad(listed, (0, PART - HALO))[:, None].astype(BF)
    columns = jnp.concatenate([forward_columns.reshape(-1), reverse_columns.reshape(-1)])
    columns = jnp.broadcast_to(columns.astype(BF)[None, :], (PART, 12))
    meta = jnp.concatenate([listed, columns, jnp.zeros((PART, HID - 13), BF)], 1)

    payload = call(
        pack_kernel, [((PART, 4 * HID), BF)], [layer_input, hidden_state, hidden_grad, meta], "pack"
    )[0]
    got = swapped(payload)
    forward_got = swapped(forward_tiles)
    reverse_got = swapped(reverse_tiles)

    def lists(width):
        return [((96, width), BF), ((96, width), BF), ((64, width), BF)]

    values, cotangent, picks, later, earlier, inner = call(
        start_kernel,
        [((PAIR, CH), BF), ((PAIR, HID), BF), ((2 * HALO, PART), BF)] + lists(CH),
        [layer_input, hidden_state, hidden_grad, meta, got],
        "start",
    )
    before, after = exchange(later, earlier)
    maps, turned = call(
        map_kernel,
        [((2 * PAIR, EXT), BF), ((2 * EXT, PAIR), BF)],
        [forward_tiles, reverse_tiles, forward_got, reverse_got, meta, got],
        "maps",
    )
    hop, later, earlier, inner = call(
        with_count(gate_hop_kernel),
        [((PAIR, 2 * CH), BF)] + lists(2 * CH),
        [values, maps, picks, before, after, inner],
        "gate_hop",
    )
    before, after = exchange(later, earlier)
    rows, gates, gated, later, earlier, inner = call(
        with_count(gate_kernel),
        [((PAIR, WIDE), BF), ((PAIR, CH), F32), ((PAIR, HID), BF)] + lists(HID),
        [values, hop, maps, picks, before, after, inner, gate_weight, gate_bias[None, :]],
        "gates",
    )
    before, after = exchange(later, earlier)
    hop, later, earlier, inner = call(
        with_count(candidate_hop_kernel),
        [((PAIR, CH), BF)] + lists(CH),
        [gated, maps, picks, before, after, inner],
        "candidate_hop",
    )
    before, after = exchange(later, earlier)
    mixed_rows, grads, later, earlier, inner = call(
        with_count(candidate_kernel),
        [((PAIR, WIDE), BF), ((PAIR, CH), BF)] + lists(CH),
        [
            rows, gated, hop, maps, turned, before, after, inner, gates, cotangent,
            candidate_weight, candidate_bias[None, :],
        ],
        "candidate",
    )
    before, after = exchange(later, earlier)
    early = call(
        candidate_sums_kernel, [((CH, WIDE), F32)], [rows, mixed_rows, grads], "candidate_sums"
    )[0]
    base, later, earlier, inner = call(
        with_count(candidate_back_kernel),
        [((PAIR, CH), F32)] + lists(CH),
        [grads, turned, picks, before, after, inner, candidate_weight],
        "candidate_back",
    )
    before, after = exchange(later, earlier)
    mixed, gate_grads, later, earlier, inner = call(
        with_count(mixed_kernel),
        [((PAIR, CH), F32), ((PAIR, CH), BF)] + lists(2 * CH),
        [base, before, after, inner, picks, turned, gates, rows, grads],
        "mixed",
    )
    half = 3 * HID // 2
    keep, send = call(
        sums_kernel,
        [((half, WIDE), F32), ((half, WIDE), BF)],
        [rows, gate_grads, early],
        "sums",
        scratch=[pltpu.VMEM((2 * half, WIDE), F32)],
    )
    before, after = exchange(later, earlier)
    samples = layer_input.shape[1] // HID * lax.axis_size("batch")
    scale = 1.0 / math.sqrt(PART * lax.axis_size("graph") * samples)
    gate_sums, gate_totals, candidate_sums, candidate_totals = total_over_all(keep, send, scale)
    base, later, earlier, inner = call(
        with_count(gate_back_kernel),
        [((PAIR, CH), F32)] + lists(CH),
        [gate_grads, turned, picks, before, after, inner, gate_weight],
        "gate_back",
    )
    before, after = exchange(later, earlier)
    keep, send = call(
        with_count(last_kernel),
        [((PART, CH), F32), ((PART, CH), F32)],
        [base, before, after, inner, picks, mixed, gates, cotangent],
        "last",
        scratch=[pltpu.VMEM((PAIR, CH), F32)],
    )
    input_total, hidden_total = call(
        place_kernel, [((PART, CH), F32), ((PART, CH), F32)], [keep, swapped(send)], "place"
    )
    return (
        input_total, hidden_total, gate_sums, gate_totals[0], candidate_sums, candidate_totals[0],
    )


def solution(mesh):
    placed = (
        P("graph", "batch"),
        P("graph", "batch"),
        P("graph", "batch"),
        P(),
        P(),
        P(),
        P(),
        P("graph", None, None, None),
        P("graph", None),
        P("graph", None, None, None),
        P("graph", None),
        P("graph", None, None),
        P("graph", None),
    )
    return jax.shard_map(
        on_device,
        mesh=mesh,
        in_specs=placed,
        out_specs=(P("graph", "batch"), P("graph", "batch"), P(), P(), P(), P()),
        check_vma=False,
    )
```

```python
import math

import jax
import jax.numpy as jnp
from jax import lax
from jax.experimental import pallas as pl
from jax.experimental.pallas import tpu as pltpu
from jax.sharding import PartitionSpec as P

HID = 64
KS = 5
CH = 128
PART = 256
PAIR = 2 * PART
HALO = 128
SLOT = 32
EXT = PART + HALO
SPAN = 2 * CH
WIDE = KS * CH + 128
BF = jnp.bfloat16
F32 = jnp.float32


def core_id():
    return lax.rem(lax.axis_index("graph"), 2)


def chip_id():
    return lax.div(lax.axis_index("graph"), 2)


def call(body, outs, args, name, flops=1 << 20, scratch=(), space=pltpu.VMEM, limit=24 << 20):
    whole = pl.BlockSpec(memory_space=pltpu.VMEM)
    return pl.pallas_call(
        body,
        out_shape=[jax.ShapeDtypeStruct(shape, dtype) for shape, dtype in outs],
        in_specs=[pl.BlockSpec(memory_space=space)] * len(args),
        out_specs=[whole] * len(outs),
        scratch_shapes=list(scratch),
        compiler_params=pltpu.CompilerParams(vmem_limit_bytes=limit),
        cost_estimate=pl.CostEstimate(flops=flops, bytes_accessed=1 << 20, transcendentals=0),
        name=name,
    )(*args)


def mm(left, right):
    return jnp.dot(left, right, preferred_element_type=F32)


def mm_t(left, right):
    return lax.dot_general(left, right, (((1,), (1,)), ((), ())), preferred_element_type=F32)


def t_mm(left, right):
    return lax.dot_general(left, right, (((0,), (0,)), ((), ())), preferred_element_type=F32)


def rows_at(index, size):
    return pl.ds(pl.multiple_of(index * size, size), size)


def sends_later():
    return (core_id() == 0) == (lax.rem(chip_id(), 2) == 0)


def from_ends(got, other, count):
    chip = chip_id()
    before = jnp.where(sends_later(), other, got)
    after = jnp.where(sends_later(), got, other)
    before = jnp.where(chip > 0, before, jnp.zeros_like(before))
    after = jnp.where(chip < count - 1, after, jnp.zeros_like(after))
    return before, after


def send_lists(picks, values, out, inner):
    out_a = mm(picks[:HALO], values[:PART]).astype(BF)
    out_b = mm(picks[HALO:], values[PART:]).astype(BF)
    out[...] = jnp.where(
        sends_later(),
        jnp.concatenate([out_a[64:96], out_b[0:32], out_b[64:96]], 0),
        jnp.concatenate([out_a[32:64], out_a[96:128], out_b[96:128]], 0),
    )
    inner[...] = jnp.concatenate([out_b[32:64], out_a[0:32]], 0)


def rims(got, other, inner, count):
    before, after = from_ends(got[...], other[...], count)
    inner = inner[...]
    rim_a = jnp.concatenate([before[32:64], inner[0:32], before[0:32], after[32:64]], 0)
    rim_b = jnp.concatenate([inner[32:64], after[0:32], before[64:96], after[64:96]], 0)
    return rim_a, rim_b


def return_lists(rim_a, rim_b, out, inner):
    rim_a = rim_a.astype(BF)
    rim_b = rim_b.astype(BF)
    out[...] = jnp.where(
        sends_later(),
        jnp.concatenate([rim_b[32:64], rim_a[96:128], rim_b[96:128]], 0),
        jnp.concatenate([rim_a[64:96], rim_a[0:32], rim_b[64:96]], 0),
    )
    inner[...] = jnp.concatenate([rim_a[32:64], rim_b[0:32]], 0)


def arrivals(got, other, inner, count):
    before, after = from_ends(got[...], other[...], count)
    inner = inner[...]
    to_a = jnp.concatenate([inner[32:64], before[0:32], after[0:32], before[32:64]], 0)
    to_b = jnp.concatenate([after[32:64], inner[0:32], after[64:96], before[64:96]], 0)
    return to_a, to_b


def load_kernel(
    x_ref, h_ref, c_ref, rows_ref, count_ref, fc_ref, rc_ref,
    own_ref, listed, counts, f_columns, r_columns, sems,
):
    inputs = (
        (rows_ref, listed), (count_ref, counts), (fc_ref, f_columns), (rc_ref, r_columns),
        (x_ref, own_ref.at[:, 0:CH]), (h_ref, own_ref.at[:, CH : 2 * CH]),
        (c_ref, own_ref.at[:, 2 * CH : 3 * CH]),
    )
    copies = [
        pltpu.make_async_copy(source, target, sems.at[k])
        for k, (source, target) in enumerate(inputs)
    ]
    for copy in copies:
        copy.start()
    for copy in copies[:4]:
        copy.wait()
    across = lax.broadcasted_iota(jnp.int32, (SLOT, SLOT), 1)
    down = lax.broadcasted_iota(jnp.int32, (SLOT, SLOT), 0)
    lists = []
    for j in range(4):
        row = jnp.where(across < counts[0:1, j : j + 1], listed[0, j : j + 1, :], -1)
        lists.append(
            jnp.sum(jnp.where(across == down, row.astype(F32), 0.0), axis=1, keepdims=True)
        )
    lanes = lax.broadcasted_iota(jnp.int32, (HALO, CH), 1)
    meta = jnp.where(lanes == 0, jnp.concatenate(lists, 0), 0.0)
    for way, ref in enumerate((f_columns, r_columns)):
        for row in range(2):
            for t in range(3):
                value = ref[row : row + 1, t : t + 1].astype(F32)
                meta = jnp.where(lanes == 1 + way * 6 + row * 3 + t, value, meta)
    own_ref[:HALO, 3 * CH :] = meta.astype(BF)
    own_ref[HALO:, 3 * CH :] = jnp.zeros((PART - HALO, CH), BF)
    for copy in copies[4:]:
        copy.wait()


def picks_of(row_column):
    lanes = lax.broadcasted_iota(jnp.int32, (HALO, PART), 1)
    return jnp.where(lanes == row_column.astype(F32).astype(jnp.int32), 1.0, 0.0).astype(BF)


def start_kernel(own_ref, got_ref, v_ref, cot_ref, pick_ref, out, inner):
    core = core_id()
    for slot, ref in ((core, own_ref), (1 - core, got_ref)):
        at = rows_at(slot, PART)
        v_ref[at, :] = ref[:, :SPAN]
        cot_ref[at, :] = ref[:, SPAN : SPAN + CH]
        pick_ref[rows_at(slot, HALO), :] = picks_of(ref[:HALO, 3 * CH : 3 * CH + 1])
    send_lists(pick_ref[...], v_ref[...], out, inner)


def map_kernel(own_f, own_r, got_f, got_r, own_ref, got_ref, map_ref):
    core = core_id()
    for slot, pair, ref in ((core, (own_f, own_r), own_ref), (1 - core, (got_f, got_r), got_ref)):
        columns = ref[:HALO, 3 * CH :].astype(F32)
        map_part = map_ref.at[rows_at(slot, 2 * PART), :]
        for way, tiles in enumerate(pair):
            for row in range(2):
                where_to = [columns[:, 1 + way * 6 + row * 3 + t :][:, :1] for t in range(3)]
                values = [tiles[row, t].astype(F32) for t in range(3)]
                at = way * PART + row * 128
                for block in range(3):
                    total = jnp.zeros((128, 128), F32)
                    for t in range(3):
                        total = total + jnp.where(where_to[t] == block, values[t], 0.0)
                    map_part[at : at + 128, block * 128 : block * 128 + 128] = total.astype(BF)


def turn_kernel(map_ref, turned_ref):
    for part in range(2):
        turned_ref[part * EXT : (part + 1) * EXT, :] = (
            map_ref[part * PAIR : (part + 1) * PAIR, :].astype(F32).T.astype(BF)
        )


def weight_kernel(gate_ref, candidate_ref, gate_bias, candidate_bias, wb_ref, wc_ref, bb_ref, bc_ref):
    low = lax.broadcasted_iota(jnp.int32, (HID, CH), 1) < HID
    for block in range(2 * KS):
        weight = gate_ref[block * HID : (block + 1) * HID, :].astype(F32)
        swapped_halves = pltpu.roll(weight, HID, 1)
        at = block * CH
        wb_ref[at : at + HID, :CH] = jnp.where(low, weight, 0.0).astype(BF)
        wb_ref[at : at + HID, CH:] = jnp.where(low, swapped_halves, 0.0).astype(BF)
        wb_ref[at + HID : at + CH, :CH] = jnp.where(low, 0.0, swapped_halves).astype(BF)
        wb_ref[at + HID : at + CH, CH:] = jnp.where(low, 0.0, weight).astype(BF)
    for k in range(KS):
        weight = candidate_ref[:, k * CH : (k + 1) * CH].astype(F32)
        both = jnp.concatenate([weight, weight], 0).T
        for half in range(2):
            weight = both[half * HID : (half + 1) * HID, :]
            at = k * SPAN + half * CH
            wc_ref[at : at + HID, :] = jnp.where(low, weight, 0.0).astype(BF)
            wc_ref[at + HID : at + CH, :] = jnp.where(low, 0.0, weight).astype(BF)
    bias = jnp.broadcast_to(gate_bias[...], (8, CH))
    first = lax.broadcasted_iota(jnp.int32, (8, CH), 1) < HID
    turned = pltpu.roll(bias, HID, 1)
    bb_ref[:, :CH] = jnp.where(first, bias, turned)
    bb_ref[:, CH:] = jnp.where(first, turned, bias)
    bc_ref[...] = jnp.broadcast_to(
        jnp.concatenate([candidate_bias[...], candidate_bias[...]], 1), (8, CH)
    )


def gate_hop_kernel(
    count, v_ref, map_ref, pick_ref, got, other, inner, hop_ref, out, inner_out
):
    for part, rim in enumerate(rims(got, other, inner, count)):
        at = slice(part * PART, (part + 1) * PART)
        full = jnp.concatenate([v_ref[at, :], rim], 0)
        both = mm(map_ref[part * PAIR : (part + 1) * PAIR, :], full).astype(BF)
        hop_ref[at, :SPAN] = both[:PART]
        hop_ref[at, SPAN:] = both[PART:]
    send_lists(pick_ref[...], hop_ref[...], out, inner_out)


def second_hop(part, way, width, base, hop_ref, rim, map_ref):
    at = slice(part * PART, (part + 1) * PART)
    columns = slice(way * width, (way + 1) * width)
    full = jnp.concatenate([hop_ref[at, columns], rim[:, columns]], 0)
    operator = map_ref[part * PAIR + way * PART : part * PAIR + (way + 1) * PART, :]
    return (2.0 * mm(operator, full) - base).astype(BF)


def gate_kernel(
    count, v_ref, hop_ref, map_ref, pick_ref, got, other, inner, weight_ref, bias_ref,
    rows_ref, gates_ref, gated_ref, out, inner_out,
):
    rows_ref[:, 0:SPAN] = v_ref[...]
    rows_ref[:, SPAN : 2 * SPAN] = hop_ref[:, :SPAN]
    rows_ref[:, 3 * SPAN : 4 * SPAN] = hop_ref[:, SPAN:]
    rows_ref[:, KS * SPAN :] = jnp.ones((PAIR, 128), BF)
    for part, rim in enumerate(rims(got, other, inner, count)):
        at = slice(part * PART, (part + 1) * PART)
        base = v_ref[at, :].astype(F32)
        for way in range(2):
            place = (2 + 2 * way) * SPAN
            rows_ref[at, place : place + SPAN] = second_hop(
                part, way, SPAN, base, hop_ref, rim, map_ref
            )
    gates = jax.nn.sigmoid(mm(rows_ref[:, : KS * SPAN], weight_ref[...]) + bias_ref[0:1, :])
    gates_ref[...] = gates
    gated = (gates[:, :CH] * v_ref[:, CH:].astype(F32)).astype(BF)
    gated_ref[...] = gated
    send_lists(pick_ref[...], gated, out, inner_out)


def input_part_kernel(rows_ref, weight_ref, bias_ref, out_ref):
    total = bias_ref[0:1, :]
    for k in range(KS):
        at = k * SPAN
        total = total + mm(rows_ref[:, at : at + CH], weight_ref[at : at + CH, :])
    out_ref[...] = total


def candidate_hop_kernel(
    count, gated_ref, map_ref, pick_ref, got, other, inner, turned_ref, hop_ref, out, inner_out
):
    for part, rim in enumerate(rims(got, other, inner, count)):
        at = slice(part * PART, (part + 1) * PART)
        full = jnp.concatenate([gated_ref[at, :], rim], 0)
        both = mm(map_ref[part * PAIR : (part + 1) * PAIR, :], full).astype(BF)
        hop_ref[at, :CH] = both[:PART]
        hop_ref[at, CH:] = both[PART:]
    send_lists(pick_ref[...], hop_ref[...], out, inner_out)


def back_rims(grad, width, turned_ref, out, inner_out):
    back = []
    for part in range(2):
        turned = turned_ref[part * EXT + PART : (part + 1) * EXT, :]
        mine = grad[part * PART : (part + 1) * PART]
        back.append(
            jnp.concatenate([mm(turned[:, :PART], mine), mm(turned[:, PART:], mine)], 1)
        )
    return_lists(back[0], back[1], out, inner_out)


def candidate_kernel(
    count, v_ref, gated_ref, hop_ref, map_ref, turned_ref, got, other, inner, gates_ref, cot_ref,
    input_part, weight_ref, members_ref, grads_ref, out, inner_out,
):
    members_ref[:, 0:CH] = gated_ref[...]
    members_ref[:, CH : 2 * CH] = hop_ref[:, :CH]
    members_ref[:, 3 * CH : 4 * CH] = hop_ref[:, CH:]
    for part, rim in enumerate(rims(got, other, inner, count)):
        at = slice(part * PART, (part + 1) * PART)
        base = gated_ref[at, :].astype(F32)
        for way in range(2):
            place = (2 + 2 * way) * CH
            members_ref[at, place : place + CH] = second_hop(
                part, way, CH, base, hop_ref, rim, map_ref
            )
    total = input_part[...]
    for k in range(KS):
        at = k * SPAN + CH
        total = total + mm(members_ref[:, k * CH : (k + 1) * CH], weight_ref[at : at + CH, :])
    candidate = jnp.tanh(total)
    hidden = v_ref[:, CH:].astype(F32)
    cotangent = cot_ref[...].astype(F32)
    update = gates_ref[:, CH:]
    update_grad = cotangent * (hidden - candidate)
    grad = (cotangent * (1.0 - update) * (1.0 - candidate * candidate)).astype(BF)
    grads_ref[:, :CH] = grad
    grads_ref[:, CH:] = (update_grad * update * (1.0 - update)).astype(BF)
    back_rims(grad, CH, turned_ref, out, inner_out)


def same_sample(products):
    low = lax.broadcasted_iota(jnp.int32, (HID, CH), 1) < HID
    top, bottom = products[:HID], products[HID:]
    return jnp.where(
        low,
        top[:, :CH] + pltpu.roll(bottom[:, :CH], HID, 1),
        pltpu.roll(top[:, CH:], HID, 1) + bottom[:, CH:],
    )


def gate_sums_of(grad, rows_ref, out_ref):
    products = t_mm(grad, rows_ref[...])
    for k in range(KS):
        out_ref[:, k * CH : (k + 1) * CH] = same_sample(products[:, k * SPAN : (k + 1) * SPAN])
    ones = products[:, KS * SPAN :]
    out_ref[:, KS * CH :] = ones[:HID] + ones[HID:]


def candidate_sums_kernel(rows_ref, members_ref, grads_ref, sums_ref):
    grad = grads_ref[:, :CH]
    inputs = t_mm(grad, rows_ref[...])
    hiddens = t_mm(grad, members_ref[...])
    for k in range(KS):
        products = jnp.concatenate(
            [inputs[:, k * SPAN : k * SPAN + CH], hiddens[:, k * CH : (k + 1) * CH]], 1
        )
        sums_ref[:HID, k * CH : (k + 1) * CH] = same_sample(products)
    ones = inputs[:, KS * SPAN :]
    sums_ref[:HID, KS * CH :] = ones[:HID] + ones[HID:]
    gate_sums_of(grads_ref[:, CH:], rows_ref, sums_ref.at[HID:, :])


def back_hop(
    grad, width, turned_ref, pick_ref, to_a, to_b, weight_ref, out, inner_out,
    base_ref,
):
    def product(left, k):
        return mm_t(left, weight_ref[k * SPAN : (k + 1) * SPAN, :])

    rim = []
    for part, coming in enumerate((to_a, to_b)):
        at = slice(part * PART, (part + 1) * PART)
        turned = turned_ref[part * EXT : (part + 1) * EXT, :]
        mine = grad[at]
        back = t_mm(pick_ref[part * HALO : (part + 1) * HALO, :], coming)
        pair = []
        for way in range(2):
            once = mm(turned[:PART, way * PART : (way + 1) * PART], mine)
            once = (2.0 * (once + back[:, way * width : (way + 1) * width])).astype(BF)
            pair.append((product(mine, 1 + 2 * way) + product(once, 2 + 2 * way)).astype(BF))
        spread = mm(turned, jnp.concatenate(pair, 0))
        rim.append(spread[PART:])
        base_ref[at, :] = (
            spread[:PART] + product(mine, 0) - product(mine, 2) - product(mine, 4)
        )
    return_lists(rim[0], rim[1], out, inner_out)


def back_kernel(
    count, grads_ref, turned_ref, pick_ref, got, other, inner, weight_ref, *refs
):
    base_ref, out, inner_out = refs[-3:]
    to_a, to_b = arrivals(got, other, inner, count)
    width = weight_ref.shape[1]
    back_hop(
        grads_ref[:, :width], width, turned_ref, pick_ref, to_a, to_b, weight_ref,
        out, inner_out, base_ref,
    )


def mixed_kernel(
    count, base_ref, got, other, inner, pick_ref, turned_ref, gates_ref, v_ref, grads_ref,
    early_ref, mixed_ref, gate_grads_ref, out, inner_out,
):
    for part, coming in enumerate(arrivals(got, other, inner, count)):
        at = slice(part * PART, (part + 1) * PART)
        mixed_ref[at, :] = base_ref[at, :] + t_mm(
            pick_ref[part * HALO : (part + 1) * HALO, :], coming
        )
    reset = gates_ref[:, :CH]
    grad = mixed_ref[:, CH:] * v_ref[:, CH:].astype(F32) * reset * (1.0 - reset)
    gate_grads_ref[:, :CH] = grad.astype(BF)
    gate_grads_ref[:, CH:] = grads_ref[:, CH:]
    back_rims(gate_grads_ref[...], SPAN, turned_ref, out, inner_out)


def sums_kernel(quarters, size, rows_ref, gate_grads_ref, early_ref, *rest):
    outs, all_ref = rest[:-1], rest[-1]
    me = lax.axis_index("batch")
    all_ref[:HID, :] = early_ref[:HID, :]
    gate_sums_of(gate_grads_ref[:, :CH], rows_ref, all_ref.at[HID : 2 * HID, :])
    all_ref[2 * HID :, :] = early_ref[HID:, :]
    for step in range(quarters):
        target = core_id() * quarters + lax.rem(me + step, quarters)
        outs[step][...] = all_ref[rows_at(target, size), :].astype(outs[step].dtype)


def last_kernel(
    count, base_ref, got, other, inner, pick_ref, mixed_ref, gates_ref, cot_ref, input_ref, state_ref
):
    core = core_id()
    at = rows_at(core, PART)
    to_a, to_b = arrivals(got, other, inner, count)
    coming = jnp.where(core == 0, to_a, to_b)
    total = base_ref[at, :] + t_mm(pick_ref[rows_at(core, HALO), :], coming)
    mixed = mixed_ref[at, :]
    gates = gates_ref[at, :]
    input_ref[...] = mixed[:, :CH] + total[:, :CH]
    state_ref[...] = (
        cot_ref[at, :].astype(F32) * gates[:, CH:] + mixed[:, CH:] * gates[:, :CH] + total[:, CH:]
    )


def moved(value, place):
    width = lax.axis_size("batch")
    pairs = []
    for index in range(lax.axis_size("graph") * width):
        graph, y = divmod(index, width)
        chip, core, y = place(graph // 2, graph % 2, y)
        pairs.append((index, (2 * chip + core) * width + y))
    return lax.ppermute(value, ("graph", "batch"), pairs)


def turned_by(value, steps):
    width = lax.axis_size("batch")
    return moved(value, lambda chip, core, y: (chip, core, (y + steps) % width))


def swapped(value):
    return moved(value, lambda chip, core, y: (chip, 1 - core, y))


def paired(value, partners):
    return moved(value, lambda chip, core, y: (partners[chip], core, y))


def to_neighbours(chip, core, y):
    count = lax.axis_size("graph") // 2
    if core == 0:
        return chip ^ 1, core, y
    other = chip + 1 - 2 * ((chip + 1) % 2)
    if 0 <= other < count:
        return other, core, y
    return (chip, core, y ^ 1) if lax.axis_size("batch") % 2 == 0 else (other % count, core, y)


def exchange(out):
    got = moved(out, to_neighbours)
    return got, swapped(got)


def ring_steps(length):
    if length == 8:
        return [[i ^ 1 for i in range(8)], [i ^ 2 for i in range(8)], [6, 7, 4, 5, 2, 3, 0, 1]]
    if length == 4:
        return [[1, 0, 3, 2], [3, 2, 1, 0]]
    return [[1, 0]] if length == 2 else []


def chip_steps(chips):
    ring = math.gcd(chips, 8)
    inside = [
        [chip - chip % ring + step[chip % ring] for chip in range(chips)]
        for step in ring_steps(ring)
    ]
    between = [
        [step[chip // ring] * ring + chip % ring for chip in range(chips)]
        for step in ring_steps(chips // ring)
    ]
    return inside, between


def sum_kernel(terms, count, *refs):
    total = refs[0][...].astype(F32)
    for ref in refs[1:terms]:
        total = total + ref[...].astype(F32)
    outs = refs[count:]
    outs[0][...] = total.astype(outs[0].dtype)
    for out, ref in zip(outs[1:], refs[terms:]):
        out[...] = ref[...]


def summed(terms, dtype, name, after=(), through=()):
    args = list(terms) + list(through) + list(after)
    return call(
        lambda *refs: sum_kernel(len(terms), len(args), *refs),
        [(terms[0].shape, dtype)] + [(array.shape, array.dtype) for array in through],
        args,
        name,
    )


def gathered_kernel(quarters, size, *refs):
    me = lax.axis_index("batch")
    for step in range(quarters):
        source = lax.rem(me - step + quarters, quarters)
        refs[-1][rows_at(source, size), :] = refs[step][...]


def scaled_kernel(
    scale, mine_ref, got_ref, gate_ref, gate_bias_ref, candidate_ref, candidate_bias_ref
):
    mine, got = mine_ref[...].astype(F32) * scale, got_ref[...].astype(F32) * scale
    first = core_id() == 0
    total = jnp.concatenate([jnp.where(first, mine, got), jnp.where(first, got, mine)], 0)
    candidate_ref[...] = total[:HID, : KS * CH]
    for k in range(KS):
        at = slice(k * CH, (k + 1) * CH)
        gate_ref[at, :] = total[HID:, at].T
    candidate_bias_ref[...] = total[:HID, KS * CH :].T[:1]
    gate_bias_ref[...] = total[HID:, KS * CH :].T[:1]


def whole_sum(mine, scale):
    quarters = lax.axis_size("batch")
    half = 3 * HID // 2
    around = [mine] + [turned_by(mine, step) for step in range(1, quarters)]
    mine = call(
        lambda *refs: gathered_kernel(quarters, half // quarters, *refs),
        [((half, WIDE), BF)],
        around,
        "gathered",
    )[0]
    return call(
        lambda *refs: scaled_kernel(scale, *refs),
        [((KS * CH, CH), F32), ((1, CH), F32), ((HID, KS * CH), F32), ((1, HID), F32)],
        [mine, swapped(mine)],
        "scaled",
    )


def on_device(
    layer_input,
    hidden_state,
    hidden_grad,
    gate_weight,
    gate_bias,
    candidate_weight,
    candidate_bias,
    forward_tiles,
    forward_columns,
    reverse_tiles,
    reverse_columns,
    send_rows,
    send_count,
):
    count = lax.axis_size("graph") // 2

    def with_count(body):
        return lambda *refs: body(count, *refs)

    own = call(
        load_kernel,
        [((PART, 4 * CH), BF)],
        [
            layer_input, hidden_state, hidden_grad, send_rows, send_count, forward_columns,
            reverse_columns,
        ],
        "load",
        scratch=[
            pltpu.VMEM(array.shape, jnp.int32)
            for array in (send_rows, send_count, forward_columns, reverse_columns)
        ]
        + [pltpu.SemaphoreType.DMA((7,))],
        space=pltpu.HBM,
        limit=60 << 20,
    )[0]
    own_got = swapped(own)
    forward_got = swapped(forward_tiles)
    reverse_got = swapped(reverse_tiles)

    def lists(width):
        return [((96, width), BF), ((64, width), BF)]

    values, cotangent, picks, out, inner = call(
        start_kernel,
        [((PAIR, SPAN), BF), ((PAIR, CH), BF), ((2 * HALO, PART), BF)] + lists(SPAN),
        [own, own_got],
        "start",
    )
    got, other = exchange(out)
    maps = call(
        map_kernel,
        [((2 * PAIR, EXT), BF)],
        [forward_tiles, reverse_tiles, forward_got, reverse_got, own, own_got],
        "maps",
    )[0]
    hop, out, inner = call(
        with_count(gate_hop_kernel),
        [((PAIR, 2 * SPAN), BF)] + lists(2 * SPAN),
        [values, maps, picks, got, other, inner],
        "gate_hop",
    )
    got, other = exchange(out)
    gate_blocks, candidate_blocks, gate_biases, candidate_biases = call(
        weight_kernel,
        [((KS * SPAN, SPAN), BF), ((KS * SPAN, CH), BF), ((8, SPAN), F32), ((8, CH), F32)],
        [gate_weight, candidate_weight.T, gate_bias[None, :], candidate_bias[None, :]],
        "weights",
    )
    rows, gates, gated, out, inner = call(
        with_count(gate_kernel),
        [((PAIR, KS * SPAN + 128), BF), ((PAIR, SPAN), F32), ((PAIR, CH), BF)] + lists(CH),
        [values, hop, maps, picks, got, other, inner, gate_blocks, gate_biases],
        "gates",
    )
    got, other = exchange(out)
    input_part = call(
        input_part_kernel, [((PAIR, CH), F32)], [rows, candidate_blocks, candidate_biases], "inputs"
    )[0]
    turned = call(turn_kernel, [((2 * EXT, PAIR), BF)], [maps], "turn")[0]
    hop, out, inner = call(
        with_count(candidate_hop_kernel),
        [((PAIR, SPAN), BF)] + lists(SPAN),
        [gated, maps, picks, got, other, inner, turned],
        "candidate_hop",
    )
    got, other = exchange(out)
    members, grads, out, inner = call(
        with_count(candidate_kernel),
        [((PAIR, KS * CH), BF), ((PAIR, SPAN), BF)] + lists(SPAN),
        [
            values, gated, hop, maps, turned, got, other, inner, gates, cotangent, input_part,
            candidate_blocks,
        ],
        "candidate",
    )
    got, other = exchange(out)
    early = call(
        candidate_sums_kernel, [((CH, WIDE), F32)], [rows, members, grads], "candidate_sums"
    )[0]
    base, out, inner = call(
        with_count(back_kernel),
        [((PAIR, SPAN), F32)] + lists(SPAN),
        [grads, turned, picks, got, other, inner, candidate_blocks],
        "candidate_back",
    )
    got, other = exchange(out)
    mixed, gate_grads, out, inner = call(
        with_count(mixed_kernel),
        [((PAIR, SPAN), F32), ((PAIR, SPAN), BF)] + lists(2 * SPAN),
        [base, got, other, inner, picks, turned, gates, values, grads, early],
        "mixed",
    )
    quarters = lax.axis_size("batch")
    size = 3 * HID // 2 // quarters
    pieces = call(
        lambda *refs: sums_kernel(quarters, size, *refs),
        [((size, WIDE), F32)] + [((size, WIDE), BF)] * (quarters - 1),
        [rows, gate_grads, early],
        "sums",
        scratch=[pltpu.VMEM((3 * HID, WIDE), F32)],
    )
    inside, between = chip_steps(count)
    steps = inside + between
    kinds = [F32] + [BF] * (len(inside) - 1) + [F32] * len(between) + [BF]
    pieces = [pieces[0]] + [turned_by(pieces[k], k) for k in range(1, quarters)]
    mine, out = summed(pieces, kinds[0], "joined", through=[out])
    near = moved(out, to_neighbours)
    mine, near = summed([mine, paired(mine, steps[0])], kinds[1], "pair_sum", through=[near])
    far = swapped(near)
    mine = summed([mine, paired(mine, steps[1])], kinds[2], "pair_sum", after=[far])[0]
    base, out, inner = call(
        with_count(back_kernel),
        [((PAIR, SPAN), F32)] + lists(SPAN),
        [gate_grads, turned, picks, near, far, inner, gate_blocks],
        "gate_back",
    )
    near = None
    far = None
    for number, (partners, kind) in enumerate(zip(steps[2:], kinds[3:])):
        terms = [mine, paired(mine, partners)]
        if number == 0:
            mine, out = summed(terms, kind, "pair_sum", through=[out])
            near = moved(out, to_neighbours)
        elif number == 1:
            mine, near = summed(terms, kind, "pair_sum", through=[near])
            far = swapped(near)
        else:
            mine = summed(terms, kind, "pair_sum", after=[far])[0]
    if near is None:
        near = moved(out, to_neighbours)
    if far is None:
        far = swapped(near)
    input_total, hidden_total = call(
        with_count(last_kernel),
        [((PART, CH), F32), ((PART, CH), F32)],
        [base, near, far, inner, picks, mixed, gates, cotangent],
        "last",
    )

    samples = layer_input.shape[1] // HID * quarters
    scale = 1.0 / math.sqrt(PART * lax.axis_size("graph") * samples)
    gate_sums, gate_totals, candidate_sums, candidate_totals = whole_sum(mine, scale)
    return (
        input_total, hidden_total, gate_sums, gate_totals.reshape(-1), candidate_sums.T,
        candidate_totals.reshape(-1),
    )


def solution(mesh):
    placed = (
        P("graph", "batch"),
        P("graph", "batch"),
        P("graph", "batch"),
        P(),
        P(),
        P(),
        P(),
        P("graph", None, None, None),
        P("graph", None),
        P("graph", None, None, None),
        P("graph", None),
        P("graph", None, None),
        P("graph", None),
    )
    return jax.shard_map(
        on_device,
        mesh=mesh,
        in_specs=placed,
        out_specs=(P("graph", "batch"), P("graph", "batch"), P(), P(), P(), P()),
        check_vma=False,
    )
```

```python
import math

import jax
import jax.numpy as jnp
from jax import lax
from jax.experimental import pallas as pl
from jax.experimental.pallas import tpu as pltpu
from jax.sharding import PartitionSpec as P

HID = 64
KS = 5
CH = 128
PART = 256
PAIR = 2 * PART
HALO = 128
SLOT = 32
EXT = PART + HALO
SPAN = 2 * CH
WIDE = KS * CH + 128
BF = jnp.bfloat16
F32 = jnp.float32


def core_id():
    return lax.rem(lax.axis_index("graph"), 2)


def chip_id():
    return lax.div(lax.axis_index("graph"), 2)


def call(body, outs, args, name, flops=1 << 20, scratch=(), space=pltpu.VMEM, limit=24 << 20):
    whole = pl.BlockSpec(memory_space=pltpu.VMEM)
    return pl.pallas_call(
        body,
        out_shape=[jax.ShapeDtypeStruct(shape, dtype) for shape, dtype in outs],
        in_specs=[pl.BlockSpec(memory_space=space)] * len(args),
        out_specs=[whole] * len(outs),
        scratch_shapes=list(scratch),
        compiler_params=pltpu.CompilerParams(vmem_limit_bytes=limit),
        cost_estimate=pl.CostEstimate(flops=flops, bytes_accessed=1 << 20, transcendentals=0),
        name=name,
    )(*args)


def mm(left, right):
    return jnp.dot(left, right, preferred_element_type=F32)


def mm_t(left, right):
    return lax.dot_general(left, right, (((1,), (1,)), ((), ())), preferred_element_type=F32)


def t_mm(left, right):
    return lax.dot_general(left, right, (((0,), (0,)), ((), ())), preferred_element_type=F32)


def rows_at(index, size):
    return pl.ds(pl.multiple_of(index * size, size), size)


def sends_later():
    return (core_id() == 0) == (lax.rem(chip_id(), 2) == 0)


def from_ends(got, other, count):
    chip = chip_id()
    before = jnp.where(sends_later(), other, got)
    after = jnp.where(sends_later(), got, other)
    before = jnp.where(chip > 0, before, jnp.zeros_like(before))
    after = jnp.where(chip < count - 1, after, jnp.zeros_like(after))
    return before, after


def send_lists(picks, values, out, inner):
    out_a = mm(picks[:HALO], values[:PART]).astype(BF)
    out_b = mm(picks[HALO:], values[PART:]).astype(BF)
    out[...] = jnp.where(
        sends_later(),
        jnp.concatenate([out_a[64:96], out_b[0:32], out_b[64:96]], 0),
        jnp.concatenate([out_a[32:64], out_a[96:128], out_b[96:128]], 0),
    )
    inner[...] = jnp.concatenate([out_b[32:64], out_a[0:32]], 0)


def rims(got, other, inner, count):
    before, after = from_ends(got[...], other[...], count)
    inner = inner[...]
    rim_a = jnp.concatenate([before[32:64], inner[0:32], before[0:32], after[32:64]], 0)
    rim_b = jnp.concatenate([inner[32:64], after[0:32], before[64:96], after[64:96]], 0)
    return rim_a, rim_b


def both_returns(rim_a, rim_b):
    rim_a = rim_a.astype(BF)
    rim_b = rim_b.astype(BF)
    later = jnp.concatenate([rim_b[32:64], rim_a[96:128], rim_b[96:128]], 0)
    earlier = jnp.concatenate([rim_a[64:96], rim_a[0:32], rim_b[64:96]], 0)
    return later, earlier, jnp.concatenate([rim_a[32:64], rim_b[0:32]], 0)


def return_lists(rim_a, rim_b, out, inner):
    later, earlier, inside = both_returns(rim_a, rim_b)
    out[...] = jnp.where(sends_later(), later, earlier)
    inner[...] = inside


def return_both(rim_a, rim_b, first, second, inner):
    later, earlier, inside = both_returns(rim_a, rim_b)
    even = lax.rem(chip_id(), 2) == 0
    first[...] = jnp.where(even, later, earlier)
    second[...] = jnp.where(even, earlier, later)
    inner[...] = inside


def arrivals(got, other, inner, count):
    before, after = from_ends(got[...], other[...], count)
    inner = inner[...]
    to_a = jnp.concatenate([inner[32:64], before[0:32], after[0:32], before[32:64]], 0)
    to_b = jnp.concatenate([after[32:64], inner[0:32], after[64:96], before[64:96]], 0)
    return to_a, to_b


def load_kernel(
    x_ref, h_ref, c_ref, rows_ref, count_ref, fc_ref, rc_ref,
    own_ref, listed, counts, f_columns, r_columns, sems,
):
    inputs = (
        (rows_ref, listed), (count_ref, counts), (fc_ref, f_columns), (rc_ref, r_columns),
        (x_ref, own_ref.at[:, 0:CH]), (h_ref, own_ref.at[:, CH : 2 * CH]),
        (c_ref, own_ref.at[:, 2 * CH : 3 * CH]),
    )
    copies = [
        pltpu.make_async_copy(source, target, sems.at[k])
        for k, (source, target) in enumerate(inputs)
    ]
    for copy in copies:
        copy.start()
    for copy in copies[:4]:
        copy.wait()
    across = lax.broadcasted_iota(jnp.int32, (SLOT, SLOT), 1)
    down = lax.broadcasted_iota(jnp.int32, (SLOT, SLOT), 0)
    lists = []
    for j in range(4):
        row = jnp.where(across < counts[0:1, j : j + 1], listed[0, j : j + 1, :], -1)
        lists.append(
            jnp.sum(jnp.where(across == down, row.astype(F32), 0.0), axis=1, keepdims=True)
        )
    lanes = lax.broadcasted_iota(jnp.int32, (HALO, CH), 1)
    meta = jnp.where(lanes == 0, jnp.concatenate(lists, 0), 0.0)
    for way, ref in enumerate((f_columns, r_columns)):
        for row in range(2):
            for t in range(3):
                value = ref[row : row + 1, t : t + 1].astype(F32)
                meta = jnp.where(lanes == 1 + way * 6 + row * 3 + t, value, meta)
    own_ref[:HALO, 3 * CH :] = meta.astype(BF)
    own_ref[HALO:, 3 * CH :] = jnp.zeros((PART - HALO, CH), BF)
    for copy in copies[4:]:
        copy.wait()


def picks_of(row_column):
    lanes = lax.broadcasted_iota(jnp.int32, (HALO, PART), 1)
    return jnp.where(lanes == row_column.astype(F32).astype(jnp.int32), 1.0, 0.0).astype(BF)


def start_kernel(own_ref, got_ref, v_ref, cot_ref, pick_ref, out, inner):
    core = core_id()
    for slot, ref in ((core, own_ref), (1 - core, got_ref)):
        at = rows_at(slot, PART)
        v_ref[at, :] = ref[:, :SPAN]
        cot_ref[at, :] = ref[:, SPAN : SPAN + CH]
        pick_ref[rows_at(slot, HALO), :] = picks_of(ref[:HALO, 3 * CH : 3 * CH + 1])
    send_lists(pick_ref[...], v_ref[...], out, inner)


def map_kernel(own_f, own_r, got_f, got_r, own_ref, got_ref, map_ref):
    core = core_id()
    for slot, pair, ref in ((core, (own_f, own_r), own_ref), (1 - core, (got_f, got_r), got_ref)):
        columns = ref[:HALO, 3 * CH :].astype(F32)
        map_part = map_ref.at[rows_at(slot, 2 * PART), :]
        for way, tiles in enumerate(pair):
            for row in range(2):
                where_to = [columns[:, 1 + way * 6 + row * 3 + t :][:, :1] for t in range(3)]
                values = [tiles[row, t].astype(F32) for t in range(3)]
                at = way * PART + row * 128
                for block in range(3):
                    total = jnp.zeros((128, 128), F32)
                    for t in range(3):
                        total = total + jnp.where(where_to[t] == block, values[t], 0.0)
                    map_part[at : at + 128, block * 128 : block * 128 + 128] = total.astype(BF)


def turn_kernel(map_ref, turned_ref):
    for part in range(2):
        turned_ref[part * EXT : (part + 1) * EXT, :] = (
            map_ref[part * PAIR : (part + 1) * PAIR, :].astype(F32).T.astype(BF)
        )


def weight_kernel(gate_ref, candidate_ref, gate_bias, candidate_bias, wb_ref, wc_ref, bb_ref, bc_ref):
    low = lax.broadcasted_iota(jnp.int32, (HID, CH), 1) < HID
    for block in range(2 * KS):
        weight = gate_ref[block * HID : (block + 1) * HID, :].astype(F32)
        swapped_halves = pltpu.roll(weight, HID, 1)
        at = block * CH
        wb_ref[at : at + HID, :CH] = jnp.where(low, weight, 0.0).astype(BF)
        wb_ref[at : at + HID, CH:] = jnp.where(low, swapped_halves, 0.0).astype(BF)
        wb_ref[at + HID : at + CH, :CH] = jnp.where(low, 0.0, swapped_halves).astype(BF)
        wb_ref[at + HID : at + CH, CH:] = jnp.where(low, 0.0, weight).astype(BF)
    for k in range(KS):
        weight = candidate_ref[:, k * CH : (k + 1) * CH].astype(F32)
        both = jnp.concatenate([weight, weight], 0).T
        for half in range(2):
            weight = both[half * HID : (half + 1) * HID, :]
            at = k * SPAN + half * CH
            wc_ref[at : at + HID, :] = jnp.where(low, weight, 0.0).astype(BF)
            wc_ref[at + HID : at + CH, :] = jnp.where(low, 0.0, weight).astype(BF)
    bias = jnp.broadcast_to(gate_bias[...], (8, CH))
    first = lax.broadcasted_iota(jnp.int32, (8, CH), 1) < HID
    turned = pltpu.roll(bias, HID, 1)
    bb_ref[:, :CH] = jnp.where(first, bias, turned)
    bb_ref[:, CH:] = jnp.where(first, turned, bias)
    bc_ref[...] = jnp.broadcast_to(
        jnp.concatenate([candidate_bias[...], candidate_bias[...]], 1), (8, CH)
    )


def gate_hop_kernel(
    count, v_ref, map_ref, pick_ref, got, other, inner, hop_ref, out, inner_out
):
    for part, rim in enumerate(rims(got, other, inner, count)):
        at = slice(part * PART, (part + 1) * PART)
        full = jnp.concatenate([v_ref[at, :], rim], 0)
        both = mm(map_ref[part * PAIR : (part + 1) * PAIR, :], full).astype(BF)
        hop_ref[at, :SPAN] = both[:PART]
        hop_ref[at, SPAN:] = both[PART:]
    send_lists(pick_ref[...], hop_ref[...], out, inner_out)


def second_hop(part, way, width, base, hop_ref, rim, map_ref):
    at = slice(part * PART, (part + 1) * PART)
    columns = slice(way * width, (way + 1) * width)
    full = jnp.concatenate([hop_ref[at, columns], rim[:, columns]], 0)
    operator = map_ref[part * PAIR + way * PART : part * PAIR + (way + 1) * PART, :]
    return (2.0 * mm(operator, full) - base).astype(BF)


def gate_kernel(
    count, v_ref, hop_ref, map_ref, pick_ref, got, other, inner, weight_ref, bias_ref,
    rows_ref, gates_ref, gated_ref, out, inner_out,
):
    rows_ref[:, 0:SPAN] = v_ref[...]
    rows_ref[:, SPAN : 2 * SPAN] = hop_ref[:, :SPAN]
    rows_ref[:, 3 * SPAN : 4 * SPAN] = hop_ref[:, SPAN:]
    rows_ref[:, KS * SPAN :] = jnp.ones((PAIR, 128), BF)
    for part, rim in enumerate(rims(got, other, inner, count)):
        at = slice(part * PART, (part + 1) * PART)
        base = v_ref[at, :].astype(F32)
        for way in range(2):
            place = (2 + 2 * way) * SPAN
            rows_ref[at, place : place + SPAN] = second_hop(
                part, way, SPAN, base, hop_ref, rim, map_ref
            )
    gates = jax.nn.sigmoid(mm(rows_ref[:, : KS * SPAN], weight_ref[...]) + bias_ref[0:1, :])
    gates_ref[...] = gates
    gated = (gates[:, :CH] * v_ref[:, CH:].astype(F32)).astype(BF)
    gated_ref[...] = gated
    send_lists(pick_ref[...], gated, out, inner_out)


def input_part_kernel(rows_ref, weight_ref, bias_ref, out_ref):
    total = bias_ref[0:1, :]
    for k in range(KS):
        at = k * SPAN
        total = total + mm(rows_ref[:, at : at + CH], weight_ref[at : at + CH, :])
    out_ref[...] = total


def candidate_hop_kernel(
    count, gated_ref, map_ref, pick_ref, got, other, inner, turned_ref, hop_ref, out, inner_out
):
    for part, rim in enumerate(rims(got, other, inner, count)):
        at = slice(part * PART, (part + 1) * PART)
        full = jnp.concatenate([gated_ref[at, :], rim], 0)
        both = mm(map_ref[part * PAIR : (part + 1) * PAIR, :], full).astype(BF)
        hop_ref[at, :CH] = both[:PART]
        hop_ref[at, CH:] = both[PART:]
    send_lists(pick_ref[...], hop_ref[...], out, inner_out)


def back_rims(grad, turned_ref):
    back = []
    for part in range(2):
        turned = turned_ref[part * EXT + PART : (part + 1) * EXT, :]
        mine = grad[part * PART : (part + 1) * PART]
        back.append(
            jnp.concatenate([mm(turned[:, :PART], mine), mm(turned[:, PART:], mine)], 1)
        )
    return back


def candidate_kernel(
    count, v_ref, gated_ref, hop_ref, map_ref, turned_ref, got, other, inner, gates_ref, cot_ref,
    input_part, weight_ref, members_ref, grads_ref, out, inner_out,
):
    members_ref[:, 0:CH] = gated_ref[...]
    members_ref[:, CH : 2 * CH] = hop_ref[:, :CH]
    members_ref[:, 3 * CH : 4 * CH] = hop_ref[:, CH:]
    for part, rim in enumerate(rims(got, other, inner, count)):
        at = slice(part * PART, (part + 1) * PART)
        base = gated_ref[at, :].astype(F32)
        for way in range(2):
            place = (2 + 2 * way) * CH
            members_ref[at, place : place + CH] = second_hop(
                part, way, CH, base, hop_ref, rim, map_ref
            )
    total = input_part[...]
    for k in range(KS):
        at = k * SPAN + CH
        total = total + mm(members_ref[:, k * CH : (k + 1) * CH], weight_ref[at : at + CH, :])
    candidate = jnp.tanh(total)
    hidden = v_ref[:, CH:].astype(F32)
    cotangent = cot_ref[...].astype(F32)
    update = gates_ref[:, CH:]
    update_grad = cotangent * (hidden - candidate)
    grad = (cotangent * (1.0 - update) * (1.0 - candidate * candidate)).astype(BF)
    grads_ref[:, :CH] = grad
    grads_ref[:, CH:] = (update_grad * update * (1.0 - update)).astype(BF)
    return_lists(*back_rims(grad, turned_ref), out, inner_out)


def same_sample(products):
    low = lax.broadcasted_iota(jnp.int32, (HID, CH), 1) < HID
    top, bottom = products[:HID], products[HID:]
    return jnp.where(
        low,
        top[:, :CH] + pltpu.roll(bottom[:, :CH], HID, 1),
        pltpu.roll(top[:, CH:], HID, 1) + bottom[:, CH:],
    )


def gate_sums_of(grad, rows_ref, out_ref):
    products = t_mm(grad, rows_ref[...])
    for k in range(KS):
        out_ref[:, k * CH : (k + 1) * CH] = same_sample(products[:, k * SPAN : (k + 1) * SPAN])
    ones = products[:, KS * SPAN :]
    out_ref[:, KS * CH :] = ones[:HID] + ones[HID:]


def candidate_sums_kernel(rows_ref, members_ref, grads_ref, sums_ref):
    grad = grads_ref[:, :CH]
    inputs = t_mm(grad, rows_ref[...])
    hiddens = t_mm(grad, members_ref[...])
    for k in range(KS):
        products = jnp.concatenate(
            [inputs[:, k * SPAN : k * SPAN + CH], hiddens[:, k * CH : (k + 1) * CH]], 1
        )
        sums_ref[:HID, k * CH : (k + 1) * CH] = same_sample(products)
    ones = inputs[:, KS * SPAN :]
    sums_ref[:HID, KS * CH :] = ones[:HID] + ones[HID:]
    gate_sums_of(grads_ref[:, CH:], rows_ref, sums_ref.at[HID:, :])


def back_hop(grad, width, turned_ref, pick_ref, to_a, to_b, weight_ref, base_ref):
    def product(left, k):
        return mm_t(left, weight_ref[k * SPAN : (k + 1) * SPAN, :])

    rim = []
    for part, coming in enumerate((to_a, to_b)):
        at = slice(part * PART, (part + 1) * PART)
        turned = turned_ref[part * EXT : (part + 1) * EXT, :]
        mine = grad[at]
        back = t_mm(pick_ref[part * HALO : (part + 1) * HALO, :], coming)
        pair = []
        for way in range(2):
            once = mm(turned[:PART, way * PART : (way + 1) * PART], mine)
            once = (2.0 * (once + back[:, way * width : (way + 1) * width])).astype(BF)
            pair.append((product(mine, 1 + 2 * way) + product(once, 2 + 2 * way)).astype(BF))
        spread = mm(turned, jnp.concatenate(pair, 0))
        rim.append(spread[PART:])
        base_ref[at, :] = (
            spread[:PART] + product(mine, 0) - product(mine, 2) - product(mine, 4)
        )
    return rim


def back_kernel(
    count, grads_ref, turned_ref, pick_ref, got, other, inner, weight_ref, base_ref, out, inner_out
):
    to_a, to_b = arrivals(got, other, inner, count)
    rim = back_hop(
        grads_ref[:, :CH], CH, turned_ref, pick_ref, to_a, to_b, weight_ref, base_ref
    )
    return_lists(rim[0], rim[1], out, inner_out)


def arrivals_of_pairs(first, second, inner, count):
    got = jnp.where(core_id() == 0, first, second)
    other = jnp.where(core_id() == 0, second, first)
    return arrivals(got, other, inner, count)


def mixed_kernel(
    count, base_ref, got, other, inner, pick_ref, turned_ref, gates_ref, v_ref, grads_ref,
    early_ref, mixed_ref, gate_grads_ref, first_out, second_out, inner_out,
):
    for part, coming in enumerate(arrivals(got, other, inner, count)):
        at = slice(part * PART, (part + 1) * PART)
        mixed_ref[at, :] = base_ref[at, :] + t_mm(
            pick_ref[part * HALO : (part + 1) * HALO, :], coming
        )
    reset = gates_ref[:, :CH]
    grad = mixed_ref[:, CH:] * v_ref[:, CH:].astype(F32) * reset * (1.0 - reset)
    gate_grads_ref[:, :CH] = grad.astype(BF)
    gate_grads_ref[:, CH:] = grads_ref[:, CH:]
    return_both(
        *back_rims(gate_grads_ref[...], turned_ref), first_out, second_out, inner_out
    )


def folded(piece):
    return jnp.concatenate([piece[:, : WIDE // 2], piece[:, WIDE // 2 :]], 0)


def sums_kernel(
    quarters, size, rows_ref, gate_grads_ref, early_ref, first_ref, second_ref, own_ref, *rest
):
    outs, all_ref = rest[:-1], rest[-1]

    @pl.when(core_id() == 0)
    def _():
        for out, ref in zip(outs, (first_ref, second_ref)):
            out[0:96, :] = ref[...]

    @pl.when(core_id() == 1)
    def _():
        me = lax.axis_index("batch")
        all_ref[:HID, :] = early_ref[:HID, :]
        gate_sums_of(gate_grads_ref[:, :CH], rows_ref, all_ref.at[HID : 2 * HID, :])
        all_ref[2 * HID :, :] = early_ref[HID:, :]
        own_ref[...] = folded(all_ref[rows_at(me, size), :])
        for step in range(1, quarters):
            piece = all_ref[rows_at(lax.rem(me + step, quarters), size), :]
            outs[step - 1][0 : 2 * size, 0 : WIDE // 2] = folded(piece).astype(BF)


def arrived_kernel(quarters, size, own_ref, *refs):
    got, out = refs[:-1], refs[-1]

    @pl.when(core_id() == 1)
    def _():
        total = own_ref[...]
        for ref in got[: quarters - 1]:
            total = total + ref[0 : 2 * size, 0 : WIDE // 2].astype(F32)
        out[0 : 2 * size, 0 : WIDE // 2] = total.astype(BF)


def gate_back_kernel(
    count, first_got, second_got, inner, grads_ref, turned_ref, pick_ref, weight_ref,
    first_out, second_out, inner_out, base_ref,
):
    @pl.when(core_id() == 0)
    def _():
        to_a, to_b = arrivals_of_pairs(first_got[0:96, :], second_got[0:96, :], inner, count)
        rim = back_hop(
            grads_ref[...], SPAN, turned_ref, pick_ref, to_a, to_b, weight_ref, base_ref
        )
        return_both(rim[0], rim[1], first_out, second_out, inner_out)


def turn_kernel_of(size, mine_ref, got_ref, list_ref, out):
    @pl.when(core_id() == 0)
    def _():
        out[0:96, 0:SPAN] = list_ref[...]

    @pl.when(core_id() == 1)
    def _():
        at = (slice(0, 2 * size), slice(0, WIDE // 2))
        out[at] = (mine_ref[at].astype(F32) + got_ref[at].astype(F32)).astype(BF)


def third_sum_kernel(size, mine_ref, got_ref, out):
    at = (slice(0, 2 * size), slice(0, WIDE // 2))
    out[...] = mine_ref[at].astype(F32) + got_ref[at].astype(F32)


def last_kernel(
    count, first_got, second_got, base_ref, inner, pick_ref, mixed_ref, gates_ref, cot_ref,
    a_ref, b_ref,
):
    @pl.when(core_id() == 0)
    def _():
        coming = arrivals_of_pairs(
            first_got[0:96, 0:SPAN], second_got[0:96, 0:SPAN], inner, count
        )
        for part, out_ref in enumerate((a_ref, b_ref)):
            at = slice(part * PART, (part + 1) * PART)
            picks = pick_ref[part * HALO : (part + 1) * HALO, :]
            total = base_ref[at, :] + t_mm(picks, coming[part])
            mixed = mixed_ref[at, :]
            gates = gates_ref[at, :]
            out_ref[:, :CH] = mixed[:, :CH] + total[:, :CH]
            out_ref[:, CH:] = (
                cot_ref[at, :].astype(F32) * gates[:, CH:]
                + mixed[:, CH:] * gates[:, :CH]
                + total[:, CH:]
            )


def moved(value, place):
    width = lax.axis_size("batch")
    pairs = []
    for index in range(lax.axis_size("graph") * width):
        graph, y = divmod(index, width)
        chip, core, y = place(graph // 2, graph % 2, y)
        pairs.append((index, (2 * chip + core) * width + y))
    return lax.ppermute(value, ("graph", "batch"), pairs)


def turned_by(value, steps):
    width = lax.axis_size("batch")
    return moved(value, lambda chip, core, y: (chip, core, (y + steps) % width))


def swapped(value):
    return moved(value, lambda chip, core, y: (chip, 1 - core, y))


def paired(value, partners):
    return moved(value, lambda chip, core, y: (partners[chip], core, y))


def to_neighbours(chip, core, y):
    count = lax.axis_size("graph") // 2
    if core == 0:
        return chip ^ 1, core, y
    other = chip + 1 - 2 * ((chip + 1) % 2)
    if 0 <= other < count:
        return other, core, y
    return (chip, core, y ^ 1) if lax.axis_size("batch") % 2 == 0 else (other % count, core, y)


def exchange(out, beside=()):
    got = moved(out, to_neighbours)
    if beside:
        got = summed([got], got.dtype, "relay", after=beside)[0]
    return got, swapped(got)


def to_first(chip, y):
    return chip ^ 1, y


def to_second(chip, y):
    chip, _, y = to_neighbours(chip, 1, y)
    return chip, y


def by_core(value, first_place, second_place):
    def place(chip, core, y):
        to_chip, to_y = (second_place if core else first_place)(chip, y)
        return to_chip, core, to_y

    return moved(value, place)


def round_batch(steps):
    width = lax.axis_size("batch")
    return lambda chip, y: (chip, (y + steps) % width)


def to_partner(partners):
    return lambda chip, y: (partners[chip], y)


def ring_steps(length):
    if length == 8:
        return [[i ^ 1 for i in range(8)], [i ^ 2 for i in range(8)], [6, 7, 4, 5, 2, 3, 0, 1]]
    if length == 4:
        return [[1, 0, 3, 2], [3, 2, 1, 0]]
    return [[1, 0]] if length == 2 else []


def chip_steps(chips):
    ring = math.gcd(chips, 8)
    inside = [
        [chip - chip % ring + step[chip % ring] for chip in range(chips)]
        for step in ring_steps(ring)
    ]
    between = [
        [step[chip // ring] * ring + chip % ring for chip in range(chips)]
        for step in ring_steps(chips // ring)
    ]
    return inside, between


def sum_kernel(terms, count, *refs):
    total = refs[0][...].astype(F32)
    for ref in refs[1:terms]:
        total = total + ref[...].astype(F32)
    outs = refs[count:]
    outs[0][...] = total.astype(outs[0].dtype)
    for out, ref in zip(outs[1:], refs[terms:]):
        out[...] = ref[...]


def summed(terms, dtype, name, after=(), through=()):
    args = list(terms) + list(through) + list(after)
    return call(
        lambda *refs: sum_kernel(len(terms), len(args), *refs),
        [(terms[0].shape, dtype)] + [(array.shape, array.dtype) for array in through],
        args,
        name,
    )


def gathered_kernel(quarters, size, *refs):
    me = lax.axis_index("batch")
    for step in range(quarters):
        source = lax.rem(me - step + quarters, quarters)
        piece = refs[step]
        refs[-1][rows_at(source, size), :] = jnp.concatenate([piece[:size], piece[size:]], 1)


def scaled_kernel(
    scale, mine_ref, got_ref, own_result, got_result,
    input_ref, state_ref, gate_ref, gate_bias_ref, candidate_ref, candidate_bias_ref,
):
    result = jnp.where(core_id() == 0, own_result[...], got_result[...])
    input_ref[...] = result[:, :CH]
    state_ref[...] = result[:, CH:]
    total = jnp.where(core_id() == 1, mine_ref[...], got_ref[...]).astype(F32) * scale
    candidate_ref[...] = total[:HID, : KS * CH]
    for k in range(KS):
        at = slice(k * CH, (k + 1) * CH)
        gate_ref[at, :] = total[HID:, at].T
    candidate_bias_ref[...] = total[:HID, KS * CH :].T[:1]
    gate_bias_ref[...] = total[HID:, KS * CH :].T[:1]


def on_device(
    layer_input,
    hidden_state,
    hidden_grad,
    gate_weight,
    gate_bias,
    candidate_weight,
    candidate_bias,
    forward_tiles,
    forward_columns,
    reverse_tiles,
    reverse_columns,
    send_rows,
    send_count,
):
    count = lax.axis_size("graph") // 2

    def with_count(body):
        return lambda *refs: body(count, *refs)

    own = call(
        load_kernel,
        [((PART, 4 * CH), BF)],
        [
            layer_input, hidden_state, hidden_grad, send_rows, send_count, forward_columns,
            reverse_columns,
        ],
        "load",
        scratch=[
            pltpu.VMEM(array.shape, jnp.int32)
            for array in (send_rows, send_count, forward_columns, reverse_columns)
        ]
        + [pltpu.SemaphoreType.DMA((7,))],
        space=pltpu.HBM,
        limit=60 << 20,
    )[0]
    own_got = swapped(own)
    forward_got = swapped(forward_tiles)
    reverse_got = swapped(reverse_tiles)

    def lists(width):
        return [((96, width), BF), ((64, width), BF)]

    values, cotangent, picks, out, inner = call(
        start_kernel,
        [((PAIR, SPAN), BF), ((PAIR, CH), BF), ((2 * HALO, PART), BF)] + lists(SPAN),
        [own, own_got],
        "start",
    )
    maps = call(
        map_kernel,
        [((2 * PAIR, EXT), BF)],
        [forward_tiles, reverse_tiles, forward_got, reverse_got, own, own_got],
        "maps",
    )[0]
    got, other = exchange(out, [maps])
    hop, out, inner = call(
        with_count(gate_hop_kernel),
        [((PAIR, 2 * SPAN), BF)] + lists(2 * SPAN),
        [values, maps, picks, got, other, inner],
        "gate_hop",
    )
    got, other = exchange(out)
    gate_blocks, candidate_blocks, gate_biases, candidate_biases = call(
        weight_kernel,
        [((KS * SPAN, SPAN), BF), ((KS * SPAN, CH), BF), ((8, SPAN), F32), ((8, CH), F32)],
        [gate_weight, candidate_weight.T, gate_bias[None, :], candidate_bias[None, :]],
        "weights",
    )
    rows, gates, gated, out, inner = call(
        with_count(gate_kernel),
        [((PAIR, KS * SPAN + 128), BF), ((PAIR, SPAN), F32), ((PAIR, CH), BF)] + lists(CH),
        [values, hop, maps, picks, got, other, inner, gate_blocks, gate_biases],
        "gates",
    )
    got, other = exchange(out)
    input_part = call(
        input_part_kernel, [((PAIR, CH), F32)], [rows, candidate_blocks, candidate_biases], "inputs"
    )[0]
    turned = call(turn_kernel, [((2 * EXT, PAIR), BF)], [maps], "turn")[0]
    hop, out, inner = call(
        with_count(candidate_hop_kernel),
        [((PAIR, SPAN), BF)] + lists(SPAN),
        [gated, maps, picks, got, other, inner, turned],
        "candidate_hop",
    )
    got, other = exchange(out)
    members, grads, out, inner = call(
        with_count(candidate_kernel),
        [((PAIR, KS * CH), BF), ((PAIR, SPAN), BF)] + lists(SPAN),
        [
            values, gated, hop, maps, turned, got, other, inner, gates, cotangent, input_part,
            candidate_blocks,
        ],
        "candidate",
    )
    got, other = exchange(out)
    early = call(
        candidate_sums_kernel, [((CH, WIDE), F32)], [rows, members, grads], "candidate_sums"
    )[0]
    base, out, inner = call(
        with_count(back_kernel),
        [((PAIR, SPAN), F32)] + lists(SPAN),
        [grads, turned, picks, got, other, inner, candidate_blocks],
        "candidate_back",
    )
    got, other = exchange(out)
    mixed, gate_grads, first, second, inner = call(
        with_count(mixed_kernel),
        [((PAIR, SPAN), F32), ((PAIR, SPAN), BF), ((96, 2 * SPAN), BF)] + lists(2 * SPAN),
        [base, got, other, inner, picks, turned, gates, values, grads, early],
        "mixed",
    )
    quarters = lax.axis_size("batch")
    size = 3 * HID // quarters
    folds = (2 * size, WIDE // 2)
    shared = (max(96, folds[0]), 2 * SPAN)
    swaps = max(quarters - 1, 2)
    own, *pieces = call(
        lambda *refs: sums_kernel(quarters, size, *refs),
        [(folds, F32)] + [(shared, BF)] * 2 + [(folds, BF)] * (swaps - 2),
        [rows, gate_grads, early, first, second],
        "sums",
        scratch=[pltpu.VMEM((3 * HID, WIDE), F32)],
    )
    ways = [to_first, to_second] + [to_first] * (swaps - 2)
    arrived = {
        k: by_core(pieces[k], ways[k], round_batch(k + 1) if k + 1 < quarters else to_first)
        for k in [1, 0] + list(range(2, swaps))
    }
    arrived = [arrived[k] for k in range(swaps)]
    inside, between = chip_steps(count)
    steps = inside + between
    shared = (max(96, folds[0]), WIDE // 2)
    mine = call(
        lambda *refs: arrived_kernel(quarters, size, *refs), [(shared, BF)], [own] + arrived,
        "arrived",
    )[0]
    got = by_core(mine, to_first, to_partner(steps[0]))
    first, second, inner, base = call(
        with_count(gate_back_kernel),
        [((96, SPAN), BF), ((96, SPAN), BF), ((64, SPAN), BF), ((PAIR, SPAN), F32)],
        arrived[:2] + [inner, gate_grads, turned, picks, gate_blocks],
        "gate_back",
    )

    def turn(mine, got, listed):
        return call(
            lambda *refs: turn_kernel_of(size, *refs), [(shared, BF)], [mine, got, listed], "turn_in"
        )[0]

    mine = turn(mine, got, first)
    first_got = by_core(mine, to_first, to_partner(steps[1]))
    mine = turn(mine, first_got, second)
    third = to_partner(steps[2]) if len(steps) > 2 else lambda chip, y: (chip ^ 1, y)
    second_got = by_core(mine, to_second, third)
    if len(steps) > 2:
        mine = call(
            lambda *refs: third_sum_kernel(size, *refs), [(folds, F32)], [mine, second_got], "third"
        )[0]
    else:
        mine = mine[: folds[0], : folds[1]].astype(F32)
    for_first, for_second = call(
        with_count(last_kernel),
        [((PART, SPAN), F32), ((PART, SPAN), F32)],
        [first_got, second_got, base, inner, picks, mixed, gates, cotangent],
        "last",
    )
    result_got = swapped(for_second)
    for number, partners in enumerate(steps[3:]):
        kind = F32 if number + 4 < len(steps) else BF
        got = by_core(mine, to_first, to_partner(partners))
        after = [result_got] if number == 1 else []
        mine = summed([mine, got], kind, "pair_sum", after=after)[0]
    mine = mine.astype(BF)
    around = {
        step: by_core(mine, to_first, round_batch(step)) if step else mine
        for step in sorted(range(quarters), key=lambda step: step != 2)
    }
    around = [around[step] for step in range(quarters)]
    mine = call(
        lambda *refs: gathered_kernel(quarters, size, *refs),
        [((3 * HID, WIDE), BF)],
        around,
        "gathered",
    )[0]
    samples = layer_input.shape[1] // HID * quarters
    scale = 1.0 / math.sqrt(PART * lax.axis_size("graph") * samples)
    input_total, hidden_total, gate_sums, gate_totals, candidate_sums, candidate_totals = call(
        lambda *refs: scaled_kernel(scale, *refs),
        [
            ((PART, CH), F32), ((PART, CH), F32), ((KS * CH, CH), F32), ((1, CH), F32),
            ((HID, KS * CH), F32), ((1, HID), F32),
        ],
        [mine, swapped(mine), for_first, result_got],
        "scaled",
    )
    return (
        input_total, hidden_total, gate_sums, gate_totals.reshape(-1), candidate_sums.T,
        candidate_totals.reshape(-1),
    )


def solution(mesh):
    placed = (
        P("graph", "batch"),
        P("graph", "batch"),
        P("graph", "batch"),
        P(),
        P(),
        P(),
        P(),
        P("graph", None, None, None),
        P("graph", None),
        P("graph", None, None, None),
        P("graph", None),
        P("graph", None, None),
        P("graph", None),
    )
    return jax.shard_map(
        on_device,
        mesh=mesh,
        in_specs=placed,
        out_specs=(P("graph", "batch"), P("graph", "batch"), P(), P(), P(), P()),
        check_vma=False,
    )
```

```python
import math

import jax
import jax.numpy as jnp
from jax import lax
from jax.experimental import pallas as pl
from jax.experimental.pallas import tpu as pltpu
from jax.sharding import PartitionSpec as P

HID = 64
KS = 5
ORDER = (0, 1, 3, 2, 4)
CH = 128
PART = 256
PAIR = 2 * PART
HALO = 128
SLOT = 32
EXT = PART + HALO
SPAN = 2 * CH
WIDE = KS * CH + 128
BF = jnp.bfloat16
F32 = jnp.float32


def core_id():
    return lax.rem(lax.axis_index("graph"), 2)


def chip_id():
    return lax.div(lax.axis_index("graph"), 2)


def call(body, outs, args, name, flops=1 << 20, scratch=(), space=pltpu.VMEM, limit=24 << 20):
    whole = pl.BlockSpec(memory_space=pltpu.VMEM)
    return pl.pallas_call(
        body,
        out_shape=[jax.ShapeDtypeStruct(shape, dtype) for shape, dtype in outs],
        in_specs=[pl.BlockSpec(memory_space=space)] * len(args),
        out_specs=[whole] * len(outs),
        scratch_shapes=list(scratch),
        compiler_params=pltpu.CompilerParams(vmem_limit_bytes=limit),
        cost_estimate=pl.CostEstimate(flops=flops, bytes_accessed=1 << 20, transcendentals=0),
        name=name,
    )(*args)


def mm(left, right):
    return jnp.dot(left, right, preferred_element_type=F32)


def mm_t(left, right):
    return lax.dot_general(left, right, (((1,), (1,)), ((), ())), preferred_element_type=F32)


def t_mm(left, right):
    return lax.dot_general(left, right, (((0,), (0,)), ((), ())), preferred_element_type=F32)


def rows_at(index, size):
    return pl.ds(pl.multiple_of(index * size, size), size)


def sends_later():
    return (core_id() == 0) == (lax.rem(chip_id(), 2) == 0)


def from_ends(got, other, count):
    chip = chip_id()
    before = jnp.where(sends_later(), other, got)
    after = jnp.where(sends_later(), got, other)
    before = jnp.where(chip > 0, before, jnp.zeros_like(before))
    after = jnp.where(chip < count - 1, after, jnp.zeros_like(after))
    return before, after


def send_lists(picks, values, out, inner):
    out_a = mm(picks[:HALO], values[:PART]).astype(BF)
    out_b = mm(picks[HALO:], values[PART:]).astype(BF)
    out[...] = jnp.where(
        sends_later(),
        jnp.concatenate([out_a[64:96], out_b[0:32], out_b[64:96]], 0),
        jnp.concatenate([out_a[32:64], out_a[96:128], out_b[96:128]], 0),
    )
    inner[...] = jnp.concatenate([out_b[32:64], out_a[0:32]], 0)


def rims(got, other, inner, count):
    before, after = from_ends(got[...], other[...], count)
    inner = inner[...]
    rim_a = jnp.concatenate([before[32:64], inner[0:32], before[0:32], after[32:64]], 0)
    rim_b = jnp.concatenate([inner[32:64], after[0:32], before[64:96], after[64:96]], 0)
    return rim_a, rim_b


def both_returns(rim_a, rim_b):
    rim_a = rim_a.astype(BF)
    rim_b = rim_b.astype(BF)
    later = jnp.concatenate([rim_b[32:64], rim_a[96:128], rim_b[96:128]], 0)
    earlier = jnp.concatenate([rim_a[64:96], rim_a[0:32], rim_b[64:96]], 0)
    return later, earlier, jnp.concatenate([rim_a[32:64], rim_b[0:32]], 0)


def return_lists(rim_a, rim_b, out, inner):
    later, earlier, inside = both_returns(rim_a, rim_b)
    out[...] = jnp.where(sends_later(), later, earlier)
    inner[...] = inside


def return_both(rim_a, rim_b, first, second, inner):
    later, earlier, inside = both_returns(rim_a, rim_b)
    even = lax.rem(chip_id(), 2) == 0
    first[...] = jnp.where(even, later, earlier)
    second[...] = jnp.where(even, earlier, later)
    inner[...] = inside


def arrivals(got, other, inner, count):
    before, after = from_ends(got[...], other[...], count)
    inner = inner[...]
    to_a = jnp.concatenate([inner[32:64], before[0:32], after[0:32], before[32:64]], 0)
    to_b = jnp.concatenate([after[32:64], inner[0:32], after[64:96], before[64:96]], 0)
    return to_a, to_b


def load_kernel(
    x_ref, h_ref, c_ref, rows_ref, count_ref, fc_ref, rc_ref,
    own_ref, listed, counts, f_columns, r_columns, sems,
):
    inputs = (
        (rows_ref, listed), (count_ref, counts), (fc_ref, f_columns), (rc_ref, r_columns),
        (x_ref, own_ref.at[:, 0:CH]), (h_ref, own_ref.at[:, CH : 2 * CH]),
        (c_ref, own_ref.at[:, 2 * CH : 3 * CH]),
    )
    copies = [
        pltpu.make_async_copy(source, target, sems.at[k])
        for k, (source, target) in enumerate(inputs)
    ]
    for copy in copies:
        copy.start()
    for copy in copies[:4]:
        copy.wait()
    across = lax.broadcasted_iota(jnp.int32, (SLOT, SLOT), 1)
    down = lax.broadcasted_iota(jnp.int32, (SLOT, SLOT), 0)
    lists = []
    for j in range(4):
        row = jnp.where(across < counts[0:1, j : j + 1], listed[0, j : j + 1, :], -1)
        lists.append(
            jnp.sum(jnp.where(across == down, row.astype(F32), 0.0), axis=1, keepdims=True)
        )
    lanes = lax.broadcasted_iota(jnp.int32, (HALO, CH), 1)
    meta = jnp.where(lanes == 0, jnp.concatenate(lists, 0), 0.0)
    for way, ref in enumerate((f_columns, r_columns)):
        for row in range(2):
            for t in range(3):
                value = ref[row : row + 1, t : t + 1].astype(F32)
                meta = jnp.where(lanes == 1 + way * 6 + row * 3 + t, value, meta)
    own_ref[:HALO, 3 * CH :] = meta.astype(BF)
    own_ref[HALO:, 3 * CH :] = jnp.zeros((PART - HALO, CH), BF)
    for copy in copies[4:]:
        copy.wait()


def picks_of(row_column):
    lanes = lax.broadcasted_iota(jnp.int32, (HALO, PART), 1)
    return jnp.where(lanes == row_column.astype(F32).astype(jnp.int32), 1.0, 0.0).astype(BF)


def start_kernel(own_ref, got_ref, v_ref, cot_ref, pick_ref, out, inner):
    core = core_id()
    for slot, ref in ((core, own_ref), (1 - core, got_ref)):
        at = rows_at(slot, PART)
        v_ref[at, :] = ref[:, :SPAN]
        cot_ref[at, :] = ref[:, SPAN : SPAN + CH]
        pick_ref[rows_at(slot, HALO), :] = picks_of(ref[:HALO, 3 * CH : 3 * CH + 1])
    send_lists(pick_ref[...], v_ref[...], out, inner)


def map_kernel(own_f, own_r, got_f, got_r, own_ref, got_ref, map_ref):
    core = core_id()
    for slot, pair, ref in ((core, (own_f, own_r), own_ref), (1 - core, (got_f, got_r), got_ref)):
        columns = ref[:HALO, 3 * CH :].astype(F32)
        map_part = map_ref.at[rows_at(slot, 2 * PART), :]
        for way, tiles in enumerate(pair):
            for row in range(2):
                where_to = [columns[:, 1 + way * 6 + row * 3 + t :][:, :1] for t in range(3)]
                values = [tiles[row, t].astype(F32) for t in range(3)]
                at = way * PART + row * 128
                for block in range(3):
                    total = jnp.zeros((128, 128), F32)
                    for t in range(3):
                        total = total + jnp.where(where_to[t] == block, values[t], 0.0)
                    map_part[at : at + 128, block * 128 : block * 128 + 128] = total.astype(BF)


def turn_kernel(map_ref, turned_ref):
    for part in range(2):
        turned_ref[part * EXT : (part + 1) * EXT, :] = (
            map_ref[part * PAIR : (part + 1) * PAIR, :].astype(F32).T.astype(BF)
        )


def weight_kernel(gate_ref, candidate_ref, gate_bias, candidate_bias, wb_ref, wc_ref, bb_ref, bc_ref, wct_ref, wc2_ref):
    low = lax.broadcasted_iota(jnp.int32, (HID, CH), 1) < HID
    for block in range(2 * KS):
        weight = gate_ref[block * HID : (block + 1) * HID, :].astype(F32)
        swapped_halves = pltpu.roll(weight, HID, 1)
        at = (2 * ORDER[block // 2] + block % 2) * CH
        wb_ref[at : at + HID, :CH] = jnp.where(low, weight, 0.0).astype(BF)
        wb_ref[at : at + HID, CH:] = jnp.where(low, swapped_halves, 0.0).astype(BF)
        wb_ref[at + HID : at + CH, :CH] = jnp.where(low, 0.0, swapped_halves).astype(BF)
        wb_ref[at + HID : at + CH, CH:] = jnp.where(low, 0.0, weight).astype(BF)
    for k in range(KS):
        weight = candidate_ref[:, k * CH : (k + 1) * CH].astype(F32)
        both = jnp.concatenate([weight, weight], 0).T
        for half in range(2):
            weight = both[half * HID : (half + 1) * HID, :]
            at = k * SPAN + half * CH
            wc_ref[at : at + HID, :] = jnp.where(low, weight, 0.0).astype(BF)
            wc_ref[at + HID : at + CH, :] = jnp.where(low, 0.0, weight).astype(BF)
        block = wc_ref[k * SPAN : (k + 1) * SPAN, :].astype(F32)
        wct_ref[k * CH : (k + 1) * CH, :] = block.T.astype(BF)
        if k in (2, 4):
            wc2_ref[(k // 2 - 1) * CH : k // 2 * CH, :] = block[CH:, :].astype(BF)
    bias = jnp.broadcast_to(gate_bias[...], (8, CH))
    first = lax.broadcasted_iota(jnp.int32, (8, CH), 1) < HID
    turned = pltpu.roll(bias, HID, 1)
    bb_ref[:, :CH] = jnp.where(first, bias, turned)
    bb_ref[:, CH:] = jnp.where(first, turned, bias)
    bc_ref[...] = jnp.broadcast_to(
        jnp.concatenate([candidate_bias[...], candidate_bias[...]], 1), (8, CH)
    )


def gate_hop_kernel(
    count, v_ref, map_ref, pick_ref, got, other, inner, hop_ref, out, inner_out
):
    for part, rim in enumerate(rims(got, other, inner, count)):
        at = slice(part * PART, (part + 1) * PART)
        full = jnp.concatenate([v_ref[at, :], rim], 0)
        both = mm(map_ref[part * PAIR : (part + 1) * PAIR, :], full).astype(BF)
        hop_ref[at, :SPAN] = both[:PART]
        hop_ref[at, SPAN:] = both[PART:]
    send_lists(pick_ref[...], hop_ref[...], out, inner_out)


def second_hop(part, way, width, base, hop_ref, rim, map_ref):
    at = slice(part * PART, (part + 1) * PART)
    columns = slice(way * width, (way + 1) * width)
    full = jnp.concatenate([hop_ref[at, columns], rim[:, columns]], 0)
    operator = map_ref[part * PAIR + way * PART : part * PAIR + (way + 1) * PART, :]
    return (2.0 * mm(operator, full) - base).astype(BF)


def gate_start_kernel(v_ref, hop_ref, weight_ref, bias_ref, out_ref):
    out_ref[...] = (
        bias_ref[0:1, :]
        + mm(v_ref[...], weight_ref[:SPAN, :])
        + mm(hop_ref[...], weight_ref[SPAN : 3 * SPAN, :])
    )


def gate_kernel(
    count, v_ref, hop_ref, map_ref, pick_ref, got, other, inner, weight_ref, start_ref,
    second_ref, gates_ref, gated_ref, out, inner_out,
):
    for part, rim in enumerate(rims(got, other, inner, count)):
        at = slice(part * PART, (part + 1) * PART)
        base = v_ref[at, :].astype(F32)
        for way in range(2):
            second_ref[at, way * SPAN : (way + 1) * SPAN] = second_hop(
                part, way, SPAN, base, hop_ref, rim, map_ref
            )
    gates = jax.nn.sigmoid(
        start_ref[...] + mm(second_ref[...], weight_ref[3 * SPAN : 5 * SPAN, :])
    )
    gates_ref[...] = gates
    gated = (gates[:, :CH] * v_ref[:, CH:].astype(F32)).astype(BF)
    gated_ref[...] = gated
    send_lists(pick_ref[...], gated, out, inner_out)


def supports_of(first_ref, hop_ref, second_ref, width):
    return (
        (first_ref, 0), (hop_ref, 0), (second_ref, 0), (hop_ref, width), (second_ref, width),
    )


def candidate_start_kernel(
    v_ref, gate_hop_ref, gate_second_ref, gated_ref, hop_ref, weight_ref, bias_ref, out_ref
):
    total = bias_ref[0:1, :]
    for k, (ref, at) in enumerate(supports_of(v_ref, gate_hop_ref, gate_second_ref, SPAN)):
        total = total + mm(ref[:, at : at + CH], weight_ref[k * SPAN : k * SPAN + CH, :])
    for k, value in ((0, gated_ref[...]), (1, hop_ref[:, :CH]), (3, hop_ref[:, CH:])):
        total = total + mm(value, weight_ref[k * SPAN + CH : (k + 1) * SPAN, :])
    out_ref[...] = total


def candidate_hop_kernel(
    count, gated_ref, map_ref, pick_ref, got, other, inner, turned_ref, hop_ref, out, inner_out
):
    for part, rim in enumerate(rims(got, other, inner, count)):
        at = slice(part * PART, (part + 1) * PART)
        full = jnp.concatenate([gated_ref[at, :], rim], 0)
        both = mm(map_ref[part * PAIR : (part + 1) * PAIR, :], full).astype(BF)
        hop_ref[at, :CH] = both[:PART]
        hop_ref[at, CH:] = both[PART:]
    send_lists(pick_ref[...], hop_ref[...], out, inner_out)


def back_rims(grad, turned_ref):
    back = []
    for part in range(2):
        turned = turned_ref[part * EXT + PART : (part + 1) * EXT, :]
        mine = grad[part * PART : (part + 1) * PART]
        back.append(
            jnp.concatenate([mm(turned[:, :PART], mine), mm(turned[:, PART:], mine)], 1)
        )
    return back


def candidate_kernel(
    count, v_ref, gated_ref, hop_ref, map_ref, turned_ref, got, other, inner, gates_ref, cot_ref,
    start_ref, weight_ref, second_ref, grads_ref, out, inner_out,
):
    for part, rim in enumerate(rims(got, other, inner, count)):
        at = slice(part * PART, (part + 1) * PART)
        base = gated_ref[at, :].astype(F32)
        for way in range(2):
            second_ref[at, way * CH : (way + 1) * CH] = second_hop(
                part, way, CH, base, hop_ref, rim, map_ref
            )
    candidate = jnp.tanh(start_ref[...] + mm(second_ref[...], weight_ref[...]))
    hidden = v_ref[:, CH:].astype(F32)
    cotangent = cot_ref[...].astype(F32)
    update = gates_ref[:, CH:]
    update_grad = cotangent * (hidden - candidate)
    grad = cotangent * (1.0 - update) * (1.0 - candidate * candidate)
    grads_ref[:, :CH] = grad.astype(BF)
    grads_ref[:, CH:] = (update_grad * update * (1.0 - update)).astype(BF)
    return_lists(*back_rims(grads_ref[:, :CH], turned_ref), out, inner_out)


def same_sample(products):
    low = lax.broadcasted_iota(jnp.int32, (HID, CH), 1) < HID
    top, bottom = products[:HID], products[HID:]
    return jnp.where(
        low,
        top[:, :CH] + pltpu.roll(bottom[:, :CH], HID, 1),
        pltpu.roll(top[:, CH:], HID, 1) + bottom[:, CH:],
    )


def totals_of(grad):
    products = t_mm(grad, jnp.ones((PAIR, 128), BF))
    return products[:HID] + products[HID:]


def gate_sums_of(grad, v_ref, hop_ref, second_ref, out_ref):
    products = [t_mm(grad, ref[...]) for ref in (v_ref, hop_ref, second_ref)]
    for k, (which, at) in enumerate(((0, 0), (1, 0), (2, 0), (1, SPAN), (2, SPAN))):
        out_ref[:, k * CH : (k + 1) * CH] = same_sample(products[which][:, at : at + SPAN])
    out_ref[:, KS * CH :] = totals_of(grad)


def candidate_sums_kernel(
    v_ref, hop_ref, second_ref, gated_ref, hidden_hop, hidden_second, grads_ref, sums_ref
):
    grad = grads_ref[:, :CH]
    supports = zip(
        supports_of(v_ref, hop_ref, second_ref, SPAN),
        supports_of(gated_ref, hidden_hop, hidden_second, CH),
    )
    for k, ((ref, at), (hidden_ref, hidden_at)) in enumerate(supports):
        products = jnp.concatenate(
            [
                t_mm(grad, ref[:, at : at + CH]),
                t_mm(grad, hidden_ref[:, hidden_at : hidden_at + CH]),
            ],
            1,
        )
        sums_ref[:HID, k * CH : (k + 1) * CH] = same_sample(products)
    sums_ref[:HID, KS * CH :] = totals_of(grad)
    gate_sums_of(grads_ref[:, CH:], v_ref, hop_ref, second_ref, sums_ref.at[HID:, :])


def back_hop(grad, width, turned_ref, pick_ref, to_a, to_b, weight_ref, base_ref):
    def product(left, k):
        return mm_t(left, weight_ref[ORDER[k] * SPAN : (ORDER[k] + 1) * SPAN, :])

    rim = []
    for part, coming in enumerate((to_a, to_b)):
        at = slice(part * PART, (part + 1) * PART)
        turned = turned_ref[part * EXT : (part + 1) * EXT, :]
        mine = grad[at]
        back = t_mm(pick_ref[part * HALO : (part + 1) * HALO, :], coming)
        pair = []
        for way in range(2):
            once = mm(turned[:PART, way * PART : (way + 1) * PART], mine)
            once = (2.0 * (once + back[:, way * width : (way + 1) * width])).astype(BF)
            pair.append((product(mine, 1 + 2 * way) + product(once, 2 + 2 * way)).astype(BF))
        spread = mm(turned, jnp.concatenate(pair, 0))
        rim.append(spread[PART:])
        base_ref[at, :] = (
            spread[:PART] + product(mine, 0) - product(mine, 2) - product(mine, 4)
        )
    return rim


def candidate_back_kernel(
    count, grads_ref, turned_ref, pick_ref, got, other, inner, weight_ref, early_ref,
    firsts_ref, out, inner_out,
):
    rim = []
    for part, coming in enumerate(arrivals(got, other, inner, count)):
        turned = turned_ref[part * EXT : (part + 1) * EXT, :]
        mine = grads_ref[part * PART : (part + 1) * PART, :CH]
        back = t_mm(pick_ref[part * HALO : (part + 1) * HALO, :], coming)
        for way in range(2):
            once = mm(turned[:PART, way * PART : (way + 1) * PART], mine)
            once = (2.0 * (once + back[:, way * CH : (way + 1) * CH])).astype(BF)
            at = (1 + 2 * way) * CH
            both = jnp.concatenate([mine, once], 1)
            row = part * PAIR + way * PART
            firsts_ref[row : row + PART, :] = mm(both, weight_ref[at : at + 2 * CH, :]).astype(BF)
        rim.append(mm(turned[PART:, :], firsts_ref[part * PAIR : (part + 1) * PAIR, :]))
    return_lists(rim[0], rim[1], out, inner_out)


def candidate_base_kernel(grads_ref, turned_ref, firsts_ref, weight_ref, base_ref):
    for part in range(2):
        at = slice(part * PART, (part + 1) * PART)
        mine = grads_ref[at, :CH]
        base_ref[at, :] = (
            mm(
                turned_ref[part * EXT : part * EXT + PART, :],
                firsts_ref[part * PAIR : (part + 1) * PAIR, :],
            )
            + mm(mine, weight_ref[0:CH, :])
            - mm(mine, weight_ref[2 * CH : 3 * CH, :])
            - mm(mine, weight_ref[4 * CH : 5 * CH, :])
        )


def arrivals_of_pairs(first, second, inner, count):
    got = jnp.where(core_id() == 0, first, second)
    other = jnp.where(core_id() == 0, second, first)
    return arrivals(got, other, inner, count)


def mixed_kernel(
    count, base_ref, got, other, inner, pick_ref, turned_ref, gates_ref, v_ref, grads_ref,
    early_ref, mixed_ref, gate_grads_ref, first_out, second_out, inner_out,
):
    for part, coming in enumerate(arrivals(got, other, inner, count)):
        at = slice(part * PART, (part + 1) * PART)
        mixed_ref[at, :] = base_ref[at, :] + t_mm(
            pick_ref[part * HALO : (part + 1) * HALO, :], coming
        )
    reset = gates_ref[:, :CH]
    grad = mixed_ref[:, CH:] * v_ref[:, CH:].astype(F32) * reset * (1.0 - reset)
    gate_grads_ref[:, :CH] = grad.astype(BF)
    gate_grads_ref[:, CH:] = grads_ref[:, CH:]
    return_both(
        *back_rims(gate_grads_ref[...], turned_ref), first_out, second_out, inner_out
    )


def folded(piece):
    return jnp.concatenate([piece[:, : WIDE // 2], piece[:, WIDE // 2 :]], 0)


def sums_kernel(
    quarters, size, v_ref, hop_ref, support_ref, gate_grads_ref, early_ref, first_ref, second_ref,
    own_ref, *rest
):
    outs, all_ref = rest[:-1], rest[-1]

    @pl.when(core_id() == 0)
    def _():
        for out, ref in zip(outs, (first_ref, second_ref)):
            out[0:96, :] = ref[...]

    @pl.when(core_id() == 1)
    def _():
        me = lax.axis_index("batch")
        all_ref[:HID, :] = early_ref[:HID, :]
        gate_sums_of(
            gate_grads_ref[:, :CH], v_ref, hop_ref, support_ref, all_ref.at[HID : 2 * HID, :]
        )
        all_ref[2 * HID :, :] = early_ref[HID:, :]
        own_ref[...] = folded(all_ref[rows_at(me, size), :])
        for step in range(1, quarters):
            piece = all_ref[rows_at(lax.rem(me + step, quarters), size), :]
            outs[step - 1][0 : 2 * size, 0 : WIDE // 2] = folded(piece).astype(BF)


def arrived_kernel(quarters, size, own_ref, *refs):
    got, out = refs[:-1], refs[-1]

    @pl.when(core_id() == 1)
    def _():
        total = own_ref[...]
        for ref in got[: quarters - 1]:
            total = total + ref[0 : 2 * size, 0 : WIDE // 2].astype(F32)
        out[0 : 2 * size, 0 : WIDE // 2] = total.astype(BF)


def gate_back_kernel(
    count, first_got, second_got, inner, grads_ref, turned_ref, pick_ref, weight_ref,
    first_out, second_out, inner_out, base_ref,
):
    @pl.when(core_id() == 0)
    def _():
        to_a, to_b = arrivals_of_pairs(first_got[0:96, :], second_got[0:96, :], inner, count)
        rim = back_hop(
            grads_ref[...], SPAN, turned_ref, pick_ref, to_a, to_b, weight_ref, base_ref
        )
        return_both(rim[0], rim[1], first_out, second_out, inner_out)


def turn_kernel_of(size, mine_ref, got_ref, list_ref, out):
    @pl.when(core_id() == 0)
    def _():
        out[0:96, 0:SPAN] = list_ref[...]

    @pl.when(core_id() == 1)
    def _():
        at = (slice(0, 2 * size), slice(0, WIDE // 2))
        out[at] = (mine_ref[at].astype(F32) + got_ref[at].astype(F32)).astype(BF)


def third_sum_kernel(size, mine_ref, got_ref, out):
    at = (slice(0, 2 * size), slice(0, WIDE // 2))
    out[...] = mine_ref[at].astype(F32) + got_ref[at].astype(F32)


def last_kernel(
    count, first_got, second_got, base_ref, inner, pick_ref, mixed_ref, gates_ref, cot_ref,
    a_ref, b_ref,
):
    @pl.when(core_id() == 0)
    def _():
        coming = arrivals_of_pairs(
            first_got[0:96, 0:SPAN], second_got[0:96, 0:SPAN], inner, count
        )
        for part, out_ref in enumerate((a_ref, b_ref)):
            at = slice(part * PART, (part + 1) * PART)
            picks = pick_ref[part * HALO : (part + 1) * HALO, :]
            total = base_ref[at, :] + t_mm(picks, coming[part])
            mixed = mixed_ref[at, :]
            gates = gates_ref[at, :]
            out_ref[:, :CH] = mixed[:, :CH] + total[:, :CH]
            out_ref[:, CH:] = (
                cot_ref[at, :].astype(F32) * gates[:, CH:]
                + mixed[:, CH:] * gates[:, :CH]
                + total[:, CH:]
            )


def moved(value, place):
    width = lax.axis_size("batch")
    pairs = []
    for index in range(lax.axis_size("graph") * width):
        graph, y = divmod(index, width)
        chip, core, y = place(graph // 2, graph % 2, y)
        pairs.append((index, (2 * chip + core) * width + y))
    return lax.ppermute(value, ("graph", "batch"), pairs)


def turned_by(value, steps):
    width = lax.axis_size("batch")
    return moved(value, lambda chip, core, y: (chip, core, (y + steps) % width))


def swapped(value):
    return moved(value, lambda chip, core, y: (chip, 1 - core, y))


def paired(value, partners):
    return moved(value, lambda chip, core, y: (partners[chip], core, y))


def to_neighbours(chip, core, y):
    count = lax.axis_size("graph") // 2
    if core == 0:
        return chip ^ 1, core, y
    other = chip + 1 - 2 * ((chip + 1) % 2)
    if 0 <= other < count:
        return other, core, y
    return (chip, core, y ^ 1) if lax.axis_size("batch") % 2 == 0 else (other % count, core, y)


def exchange(out, beside=()):
    got = moved(out, to_neighbours)
    if beside:
        got = summed([got], got.dtype, "relay", after=beside)[0]
    return got, swapped(got)


def to_first(chip, y):
    return chip ^ 1, y


def to_second(chip, y):
    chip, _, y = to_neighbours(chip, 1, y)
    return chip, y


def by_core(value, first_place, second_place):
    def place(chip, core, y):
        to_chip, to_y = (second_place if core else first_place)(chip, y)
        return to_chip, core, to_y

    return moved(value, place)


def round_batch(steps):
    width = lax.axis_size("batch")
    return lambda chip, y: (chip, (y + steps) % width)


def to_partner(partners):
    return lambda chip, y: (partners[chip], y)


def ring_steps(length):
    if length == 8:
        return [[i ^ 1 for i in range(8)], [i ^ 2 for i in range(8)], [6, 7, 4, 5, 2, 3, 0, 1]]
    if length == 4:
        return [[1, 0, 3, 2], [3, 2, 1, 0]]
    return [[1, 0]] if length == 2 else []


def chip_steps(chips):
    ring = math.gcd(chips, 8)
    inside = [
        [chip - chip % ring + step[chip % ring] for chip in range(chips)]
        for step in ring_steps(ring)
    ]
    between = [
        [step[chip // ring] * ring + chip % ring for chip in range(chips)]
        for step in ring_steps(chips // ring)
    ]
    return inside, between


def sum_kernel(terms, count, *refs):
    total = refs[0][...].astype(F32)
    for ref in refs[1:terms]:
        total = total + ref[...].astype(F32)
    outs = refs[count:]
    outs[0][...] = total.astype(outs[0].dtype)
    for out, ref in zip(outs[1:], refs[terms:]):
        out[...] = ref[...]


def summed(terms, dtype, name, after=(), through=()):
    args = list(terms) + list(through) + list(after)
    return call(
        lambda *refs: sum_kernel(len(terms), len(args), *refs),
        [(terms[0].shape, dtype)] + [(array.shape, array.dtype) for array in through],
        args,
        name,
    )


def gathered_kernel(quarters, size, *refs):
    me = lax.axis_index("batch")
    for step in range(quarters):
        source = lax.rem(me - step + quarters, quarters)
        piece = refs[step]
        refs[-1][rows_at(source, size), :] = jnp.concatenate([piece[:size], piece[size:]], 1)


def scaled_kernel(
    scale, mine_ref, got_ref, own_result, got_result,
    input_ref, state_ref, gate_ref, gate_bias_ref, candidate_ref, candidate_bias_ref,
):
    result = jnp.where(core_id() == 0, own_result[...], got_result[...])
    input_ref[...] = result[:, :CH]
    state_ref[...] = result[:, CH:]
    total = jnp.where(core_id() == 1, mine_ref[...], got_ref[...]).astype(F32) * scale
    candidate_ref[...] = total[:HID, : KS * CH]
    for k in range(KS):
        at = slice(k * CH, (k + 1) * CH)
        gate_ref[at, :] = total[HID:, at].T
    candidate_bias_ref[...] = total[:HID, KS * CH :].T[:1]
    gate_bias_ref[...] = total[HID:, KS * CH :].T[:1]


def on_device(
    layer_input,
    hidden_state,
    hidden_grad,
    gate_weight,
    gate_bias,
    candidate_weight,
    candidate_bias,
    forward_tiles,
    forward_columns,
    reverse_tiles,
    reverse_columns,
    send_rows,
    send_count,
):
    count = lax.axis_size("graph") // 2

    def with_count(body):
        return lambda *refs: body(count, *refs)

    own = call(
        load_kernel,
        [((PART, 4 * CH), BF)],
        [
            layer_input, hidden_state, hidden_grad, send_rows, send_count, forward_columns,
            reverse_columns,
        ],
        "load",
        scratch=[
            pltpu.VMEM(array.shape, jnp.int32)
            for array in (send_rows, send_count, forward_columns, reverse_columns)
        ]
        + [pltpu.SemaphoreType.DMA((7,))],
        space=pltpu.HBM,
        limit=60 << 20,
    )[0]
    own_got = swapped(own)
    forward_got = swapped(forward_tiles)
    reverse_got = swapped(reverse_tiles)

    def lists(width):
        return [((96, width), BF), ((64, width), BF)]

    values, cotangent, picks, out, inner = call(
        start_kernel,
        [((PAIR, SPAN), BF), ((PAIR, CH), BF), ((2 * HALO, PART), BF)] + lists(SPAN),
        [own, own_got],
        "start",
    )
    maps = call(
        map_kernel,
        [((2 * PAIR, EXT), BF)],
        [forward_tiles, reverse_tiles, forward_got, reverse_got, own, own_got],
        "maps",
    )[0]
    gate_blocks, candidate_blocks, gate_biases, candidate_biases, blocks_turned, two_hop_blocks = call(
        weight_kernel,
        [
            ((KS * SPAN, SPAN), BF), ((KS * SPAN, CH), BF), ((8, SPAN), F32), ((8, CH), F32),
            ((KS * CH, SPAN), BF), ((SPAN, CH), BF),
        ],
        [gate_weight, candidate_weight.T, gate_bias[None, :], candidate_bias[None, :]],
        "weights",
    )
    got, other = exchange(out, [maps, gate_biases])
    hop, out, inner = call(
        with_count(gate_hop_kernel),
        [((PAIR, 2 * SPAN), BF)] + lists(2 * SPAN),
        [values, maps, picks, got, other, inner],
        "gate_hop",
    )
    got, other = exchange(out)
    gate_start = call(
        gate_start_kernel, [((PAIR, SPAN), F32)], [values, hop, gate_blocks, gate_biases],
        "gate_start",
    )[0]
    gate_hop = hop
    gate_second, gates, gated, out, inner = call(
        with_count(gate_kernel),
        [((PAIR, 2 * SPAN), BF), ((PAIR, SPAN), F32), ((PAIR, CH), BF)] + lists(CH),
        [values, hop, maps, picks, got, other, inner, gate_blocks, gate_start],
        "gates",
    )
    got, other = exchange(out)
    turned = call(turn_kernel, [((2 * EXT, PAIR), BF)], [maps], "turn")[0]
    hop, out, inner = call(
        with_count(candidate_hop_kernel),
        [((PAIR, SPAN), BF)] + lists(SPAN),
        [gated, maps, picks, got, other, inner, turned],
        "candidate_hop",
    )
    got, other = exchange(out)
    candidate_start = call(
        candidate_start_kernel,
        [((PAIR, CH), F32)],
        [values, gate_hop, gate_second, gated, hop, candidate_blocks, candidate_biases],
        "candidate_start",
    )[0]
    second_hops, grads, out, inner = call(
        with_count(candidate_kernel),
        [((PAIR, SPAN), BF), ((PAIR, SPAN), BF)] + lists(SPAN),
        [
            values, gated, hop, maps, turned, got, other, inner, gates, cotangent, candidate_start,
            two_hop_blocks,
        ],
        "candidate",
    )
    got, other = exchange(out)
    early = call(
        candidate_sums_kernel,
        [((CH, WIDE), F32)],
        [values, gate_hop, gate_second, gated, hop, second_hops, grads],
        "candidate_sums",
    )[0]
    firsts, out, inner = call(
        with_count(candidate_back_kernel),
        [((2 * PAIR, SPAN), BF)] + lists(SPAN),
        [grads, turned, picks, got, other, inner, blocks_turned, early],
        "candidate_back",
    )
    got, other = exchange(out)
    base = call(
        candidate_base_kernel,
        [((PAIR, SPAN), F32)],
        [grads, turned, firsts, blocks_turned],
        "candidate_base",
    )[0]
    mixed, gate_grads, first, second, inner = call(
        with_count(mixed_kernel),
        [((PAIR, SPAN), F32), ((PAIR, SPAN), BF), ((96, 2 * SPAN), BF)] + lists(2 * SPAN),
        [base, got, other, inner, picks, turned, gates, values, grads, early],
        "mixed",
    )
    quarters = lax.axis_size("batch")
    size = 3 * HID // quarters
    folds = (2 * size, WIDE // 2)
    shared = (max(96, folds[0]), 2 * SPAN)
    swaps = max(quarters - 1, 2)
    own, *pieces = call(
        lambda *refs: sums_kernel(quarters, size, *refs),
        [(folds, F32)] + [(shared, BF)] * 2 + [(folds, BF)] * (swaps - 2),
        [values, gate_hop, gate_second, gate_grads, early, first, second],
        "sums",
        scratch=[pltpu.VMEM((3 * HID, WIDE), F32)],
    )
    ways = [to_first, to_second] + [to_first] * (swaps - 2)
    arrived = {
        k: by_core(pieces[k], ways[k], round_batch(k + 1) if k + 1 < quarters else to_first)
        for k in [1, 0] + list(range(2, swaps))
    }
    arrived = [arrived[k] for k in range(swaps)]
    inside, between = chip_steps(count)
    steps = inside + between
    shared = (max(96, folds[0]), WIDE // 2)
    mine = call(
        lambda *refs: arrived_kernel(quarters, size, *refs), [(shared, BF)], [own] + arrived,
        "arrived",
    )[0]
    got = by_core(mine, to_first, to_partner(steps[0]))
    first, second, inner, base = call(
        with_count(gate_back_kernel),
        [((96, SPAN), BF), ((96, SPAN), BF), ((64, SPAN), BF), ((PAIR, SPAN), F32)],
        arrived[:2] + [inner, gate_grads, turned, picks, gate_blocks],
        "gate_back",
    )

    def turn(mine, got, listed):
        return call(
            lambda *refs: turn_kernel_of(size, *refs), [(shared, BF)], [mine, got, listed], "turn_in"
        )[0]

    mine = turn(mine, got, first)
    first_got = by_core(mine, to_first, to_partner(steps[1]))
    mine = turn(mine, first_got, second)
    third = to_partner(steps[2]) if len(steps) > 2 else lambda chip, y: (chip ^ 1, y)
    second_got = by_core(mine, to_second, third)
    if len(steps) > 2:
        mine = call(
            lambda *refs: third_sum_kernel(size, *refs), [(folds, F32)], [mine, second_got], "third"
        )[0]
    else:
        mine = mine[: folds[0], : folds[1]].astype(F32)
    for_first, for_second = call(
        with_count(last_kernel),
        [((PART, SPAN), F32), ((PART, SPAN), F32)],
        [first_got, second_got, base, inner, picks, mixed, gates, cotangent],
        "last",
    )
    result_got = swapped(for_second)
    for number, partners in enumerate(steps[3:]):
        kind = F32 if number + 4 < len(steps) else BF
        got = by_core(mine, to_first, to_partner(partners))
        after = [result_got] if number == 1 else []
        mine = summed([mine, got], kind, "pair_sum", after=after)[0]
    mine = mine.astype(BF)
    around = {
        step: by_core(mine, to_first, round_batch(step)) if step else mine
        for step in sorted(range(quarters), key=lambda step: step != 2)
    }
    around = [around[step] for step in range(quarters)]
    mine = call(
        lambda *refs: gathered_kernel(quarters, size, *refs),
        [((3 * HID, WIDE), BF)],
        around,
        "gathered",
    )[0]
    samples = layer_input.shape[1] // HID * quarters
    scale = 1.0 / math.sqrt(PART * lax.axis_size("graph") * samples)
    input_total, hidden_total, gate_sums, gate_totals, candidate_sums, candidate_totals = call(
        lambda *refs: scaled_kernel(scale, *refs),
        [
            ((PART, CH), F32), ((PART, CH), F32), ((KS * CH, CH), F32), ((1, CH), F32),
            ((HID, KS * CH), F32), ((1, HID), F32),
        ],
        [mine, swapped(mine), for_first, result_got],
        "scaled",
    )
    return (
        input_total, hidden_total, gate_sums, gate_totals.reshape(-1), candidate_sums.T,
        candidate_totals.reshape(-1),
    )


def solution(mesh):
    placed = (
        P("graph", "batch"),
        P("graph", "batch"),
        P("graph", "batch"),
        P(),
        P(),
        P(),
        P(),
        P("graph", None, None, None),
        P("graph", None),
        P("graph", None, None, None),
        P("graph", None),
        P("graph", None, None),
        P("graph", None),
    )
    return jax.shard_map(
        on_device,
        mesh=mesh,
        in_specs=placed,
        out_specs=(P("graph", "batch"), P("graph", "batch"), P(), P(), P(), P()),
        check_vma=False,
    )
```

```python
import math

import jax
import jax.numpy as jnp
from jax import lax
from jax.experimental import pallas as pl
from jax.experimental.pallas import tpu as pltpu
from jax.sharding import PartitionSpec as P

HID = 64
KS = 5
ORDER = (0, 1, 3, 2, 4)
CH = 128
PART = 256
PAIR = 2 * PART
HALO = 128
SLOT = 32
EXT = PART + HALO
SPAN = 2 * CH
WIDE = KS * CH + 128
BF = jnp.bfloat16
F32 = jnp.float32


def core_id():
    return lax.rem(lax.axis_index("graph"), 2)


def chip_id():
    return lax.div(lax.axis_index("graph"), 2)


def call(body, outs, args, name, flops=1 << 20, scratch=(), space=pltpu.VMEM, limit=24 << 20):
    whole = pl.BlockSpec(memory_space=pltpu.VMEM)
    return pl.pallas_call(
        body,
        out_shape=[jax.ShapeDtypeStruct(shape, dtype) for shape, dtype in outs],
        in_specs=[pl.BlockSpec(memory_space=space)] * len(args),
        out_specs=[whole] * len(outs),
        scratch_shapes=list(scratch),
        compiler_params=pltpu.CompilerParams(vmem_limit_bytes=limit),
        cost_estimate=pl.CostEstimate(flops=flops, bytes_accessed=1 << 20, transcendentals=0),
        name=name,
    )(*args)


def mm(left, right):
    return jnp.dot(left, right, preferred_element_type=F32)


def mm_t(left, right):
    return lax.dot_general(left, right, (((1,), (1,)), ((), ())), preferred_element_type=F32)


def t_mm(left, right):
    return lax.dot_general(left, right, (((0,), (0,)), ((), ())), preferred_element_type=F32)


def rows_at(index, size):
    return pl.ds(pl.multiple_of(index * size, size), size)


def sends_later():
    return (core_id() == 0) == (lax.rem(chip_id(), 2) == 0)


def from_ends(got, other, count):
    chip = chip_id()
    before = jnp.where(sends_later(), other, got)
    after = jnp.where(sends_later(), got, other)
    before = jnp.where(chip > 0, before, jnp.zeros_like(before))
    after = jnp.where(chip < count - 1, after, jnp.zeros_like(after))
    return before, after


def send_lists(picks, values, out, inner):
    out_a = mm(picks[:HALO], values[:PART]).astype(BF)
    out_b = mm(picks[HALO:], values[PART:]).astype(BF)
    out[...] = jnp.where(
        sends_later(),
        jnp.concatenate([out_a[64:96], out_b[0:32], out_b[64:96]], 0),
        jnp.concatenate([out_a[32:64], out_a[96:128], out_b[96:128]], 0),
    )
    inner[...] = jnp.concatenate([out_b[32:64], out_a[0:32]], 0)


def rims(got, other, inner, count):
    before, after = from_ends(got[...], other[...], count)
    inner = inner[...]
    rim_a = jnp.concatenate([before[32:64], inner[0:32], before[0:32], after[32:64]], 0)
    rim_b = jnp.concatenate([inner[32:64], after[0:32], before[64:96], after[64:96]], 0)
    return rim_a, rim_b


def both_returns(rim_a, rim_b):
    rim_a = rim_a.astype(BF)
    rim_b = rim_b.astype(BF)
    later = jnp.concatenate([rim_b[32:64], rim_a[96:128], rim_b[96:128]], 0)
    earlier = jnp.concatenate([rim_a[64:96], rim_a[0:32], rim_b[64:96]], 0)
    return later, earlier, jnp.concatenate([rim_a[32:64], rim_b[0:32]], 0)


def return_lists(rim_a, rim_b, out, inner):
    later, earlier, inside = both_returns(rim_a, rim_b)
    out[...] = jnp.where(sends_later(), later, earlier)
    inner[...] = inside


def return_both(rim_a, rim_b, first, second, inner):
    later, earlier, inside = both_returns(rim_a, rim_b)
    even = lax.rem(chip_id(), 2) == 0
    first[...] = jnp.where(even, later, earlier)
    second[...] = jnp.where(even, earlier, later)
    inner[...] = inside


def arrivals(got, other, inner, count):
    before, after = from_ends(got[...], other[...], count)
    inner = inner[...]
    to_a = jnp.concatenate([inner[32:64], before[0:32], after[0:32], before[32:64]], 0)
    to_b = jnp.concatenate([after[32:64], inner[0:32], after[64:96], before[64:96]], 0)
    return to_a, to_b


def load_kernel(
    x_ref, h_ref, c_ref, rows_ref, count_ref, fc_ref, rc_ref,
    own_ref, listed, counts, f_columns, r_columns, sems,
):
    inputs = (
        (rows_ref, listed), (count_ref, counts), (fc_ref, f_columns), (rc_ref, r_columns),
        (x_ref, own_ref.at[:, 0:CH]), (h_ref, own_ref.at[:, CH : 2 * CH]),
        (c_ref, own_ref.at[:, 2 * CH : 3 * CH]),
    )
    copies = [
        pltpu.make_async_copy(source, target, sems.at[k])
        for k, (source, target) in enumerate(inputs)
    ]
    for copy in copies:
        copy.start()
    for copy in copies[:4]:
        copy.wait()
    across = lax.broadcasted_iota(jnp.int32, (SLOT, SLOT), 1)
    down = lax.broadcasted_iota(jnp.int32, (SLOT, SLOT), 0)
    lists = []
    for j in range(4):
        row = jnp.where(across < counts[0:1, j : j + 1], listed[0, j : j + 1, :], -1)
        lists.append(
            jnp.sum(jnp.where(across == down, row.astype(F32), 0.0), axis=1, keepdims=True)
        )
    lanes = lax.broadcasted_iota(jnp.int32, (HALO, CH), 1)
    meta = jnp.where(lanes == 0, jnp.concatenate(lists, 0), 0.0)
    for way, ref in enumerate((f_columns, r_columns)):
        for row in range(2):
            for t in range(3):
                value = ref[row : row + 1, t : t + 1].astype(F32)
                meta = jnp.where(lanes == 1 + way * 6 + row * 3 + t, value, meta)
    own_ref[:HALO, 3 * CH :] = meta.astype(BF)
    own_ref[HALO:, 3 * CH :] = jnp.zeros((PART - HALO, CH), BF)
    for copy in copies[4:]:
        copy.wait()


def picks_of(row_column):
    lanes = lax.broadcasted_iota(jnp.int32, (HALO, PART), 1)
    return jnp.where(lanes == row_column.astype(F32).astype(jnp.int32), 1.0, 0.0).astype(BF)


def start_kernel(own_ref, got_ref, v_ref, cot_ref, pick_ref, out, inner):
    core = core_id()
    for slot, ref in ((core, own_ref), (1 - core, got_ref)):
        at = rows_at(slot, PART)
        v_ref[at, :] = ref[:, :SPAN]
        cot_ref[at, :] = ref[:, SPAN : SPAN + CH]
        pick_ref[rows_at(slot, HALO), :] = picks_of(ref[:HALO, 3 * CH : 3 * CH + 1])
    send_lists(pick_ref[...], v_ref[...], out, inner)


def map_kernel(own_f, own_r, got_f, got_r, own_ref, got_ref, map_ref):
    core = core_id()
    for slot, pair, ref in ((core, (own_f, own_r), own_ref), (1 - core, (got_f, got_r), got_ref)):
        columns = ref[:HALO, 3 * CH :].astype(F32)
        map_part = map_ref.at[rows_at(slot, 2 * PART), :]
        for way, tiles in enumerate(pair):
            for row in range(2):
                where_to = [columns[:, 1 + way * 6 + row * 3 + t :][:, :1] for t in range(3)]
                values = [tiles[row, t].astype(F32) for t in range(3)]
                at = way * PART + row * 128
                for block in range(3):
                    total = jnp.zeros((128, 128), F32)
                    for t in range(3):
                        total = total + jnp.where(where_to[t] == block, values[t], 0.0)
                    map_part[at : at + 128, block * 128 : block * 128 + 128] = total.astype(BF)


def turn_kernel(map_ref, turned_ref):
    for part in range(2):
        turned_ref[part * EXT : (part + 1) * EXT, :] = (
            map_ref[part * PAIR : (part + 1) * PAIR, :].astype(F32).T.astype(BF)
        )


def weight_kernel(gate_ref, candidate_ref, gate_bias, candidate_bias, wb_ref, wc_ref, bb_ref, bc_ref, wct_ref, wc2_ref):
    low = lax.broadcasted_iota(jnp.int32, (HID, CH), 1) < HID
    for block in range(2 * KS):
        weight = gate_ref[block * HID : (block + 1) * HID, :].astype(F32)
        swapped_halves = pltpu.roll(weight, HID, 1)
        at = (2 * ORDER[block // 2] + block % 2) * CH
        wb_ref[at : at + HID, :CH] = jnp.where(low, weight, 0.0).astype(BF)
        wb_ref[at : at + HID, CH:] = jnp.where(low, swapped_halves, 0.0).astype(BF)
        wb_ref[at + HID : at + CH, :CH] = jnp.where(low, 0.0, swapped_halves).astype(BF)
        wb_ref[at + HID : at + CH, CH:] = jnp.where(low, 0.0, weight).astype(BF)
    for k in range(KS):
        weight = candidate_ref[:, k * CH : (k + 1) * CH].astype(F32)
        both = jnp.concatenate([weight, weight], 0).T
        for half in range(2):
            weight = both[half * HID : (half + 1) * HID, :]
            at = k * SPAN + half * CH
            wc_ref[at : at + HID, :] = jnp.where(low, weight, 0.0).astype(BF)
            wc_ref[at + HID : at + CH, :] = jnp.where(low, 0.0, weight).astype(BF)
        block = wc_ref[k * SPAN : (k + 1) * SPAN, :].astype(F32)
        wct_ref[k * CH : (k + 1) * CH, :] = block.T.astype(BF)
        if k in (2, 4):
            wc2_ref[(k // 2 - 1) * CH : k // 2 * CH, :] = block[CH:, :].astype(BF)
    bias = jnp.broadcast_to(gate_bias[...], (8, CH))
    first = lax.broadcasted_iota(jnp.int32, (8, CH), 1) < HID
    turned = pltpu.roll(bias, HID, 1)
    bb_ref[:, :CH] = jnp.where(first, bias, turned)
    bb_ref[:, CH:] = jnp.where(first, turned, bias)
    bc_ref[...] = jnp.broadcast_to(
        jnp.concatenate([candidate_bias[...], candidate_bias[...]], 1), (8, CH)
    )


def gate_hop_kernel(
    count, v_ref, map_ref, pick_ref, got, other, inner, hop_ref, out, inner_out
):
    for part, rim in enumerate(rims(got, other, inner, count)):
        at = slice(part * PART, (part + 1) * PART)
        full = jnp.concatenate([v_ref[at, :], rim], 0)
        both = mm(map_ref[part * PAIR : (part + 1) * PAIR, :], full).astype(BF)
        hop_ref[at, :SPAN] = both[:PART]
        hop_ref[at, SPAN:] = both[PART:]
    send_lists(pick_ref[...], hop_ref[...], out, inner_out)


def second_hop(part, way, width, base, hop_ref, rim, map_ref):
    at = slice(part * PART, (part + 1) * PART)
    columns = slice(way * width, (way + 1) * width)
    full = jnp.concatenate([hop_ref[at, columns], rim[:, columns]], 0)
    operator = map_ref[part * PAIR + way * PART : part * PAIR + (way + 1) * PART, :]
    return (2.0 * mm(operator, full) - base).astype(BF)


def gate_start_kernel(v_ref, hop_ref, weight_ref, bias_ref, out_ref):
    out_ref[...] = (
        bias_ref[0:1, :]
        + mm(v_ref[...], weight_ref[:SPAN, :])
        + mm(hop_ref[...], weight_ref[SPAN : 3 * SPAN, :])
    )


def gate_kernel(
    count, v_ref, hop_ref, map_ref, pick_ref, got, other, inner, weight_ref, start_ref,
    second_ref, gates_ref, gated_ref, out, inner_out,
):
    for part, rim in enumerate(rims(got, other, inner, count)):
        at = slice(part * PART, (part + 1) * PART)
        base = v_ref[at, :].astype(F32)
        for way in range(2):
            second_ref[at, way * SPAN : (way + 1) * SPAN] = second_hop(
                part, way, SPAN, base, hop_ref, rim, map_ref
            )
    gates = jax.nn.sigmoid(
        start_ref[...] + mm(second_ref[...], weight_ref[3 * SPAN : 5 * SPAN, :])
    )
    gates_ref[...] = gates
    gated = (gates[:, :CH] * v_ref[:, CH:].astype(F32)).astype(BF)
    gated_ref[...] = gated
    send_lists(pick_ref[...], gated, out, inner_out)


def supports_of(first_ref, hop_ref, second_ref, width):
    return (
        (first_ref, 0), (hop_ref, 0), (second_ref, 0), (hop_ref, width), (second_ref, width),
    )


def candidate_start_kernel(
    v_ref, gate_hop_ref, gate_second_ref, gated_ref, hop_ref, weight_ref, bias_ref, out_ref
):
    total = bias_ref[0:1, :]
    for k, (ref, at) in enumerate(supports_of(v_ref, gate_hop_ref, gate_second_ref, SPAN)):
        total = total + mm(ref[:, at : at + CH], weight_ref[k * SPAN : k * SPAN + CH, :])
    for k, value in ((0, gated_ref[...]), (1, hop_ref[:, :CH]), (3, hop_ref[:, CH:])):
        total = total + mm(value, weight_ref[k * SPAN + CH : (k + 1) * SPAN, :])
    out_ref[...] = total


def candidate_hop_kernel(
    count, gated_ref, map_ref, pick_ref, got, other, inner, turned_ref, hop_ref, out, inner_out
):
    for part, rim in enumerate(rims(got, other, inner, count)):
        at = slice(part * PART, (part + 1) * PART)
        full = jnp.concatenate([gated_ref[at, :], rim], 0)
        both = mm(map_ref[part * PAIR : (part + 1) * PAIR, :], full).astype(BF)
        hop_ref[at, :CH] = both[:PART]
        hop_ref[at, CH:] = both[PART:]
    send_lists(pick_ref[...], hop_ref[...], out, inner_out)


def back_rims(grad, turned_ref):
    back = []
    for part in range(2):
        turned = turned_ref[part * EXT + PART : (part + 1) * EXT, :]
        mine = grad[part * PART : (part + 1) * PART]
        back.append(
            jnp.concatenate([mm(turned[:, :PART], mine), mm(turned[:, PART:], mine)], 1)
        )
    return back


def candidate_kernel(
    count, v_ref, gated_ref, hop_ref, map_ref, turned_ref, got, other, inner, gates_ref, cot_ref,
    start_ref, weight_ref, second_ref, grads_ref, out, inner_out,
):
    for part, rim in enumerate(rims(got, other, inner, count)):
        at = slice(part * PART, (part + 1) * PART)
        base = gated_ref[at, :].astype(F32)
        for way in range(2):
            second_ref[at, way * CH : (way + 1) * CH] = second_hop(
                part, way, CH, base, hop_ref, rim, map_ref
            )
    candidate = jnp.tanh(start_ref[...] + mm(second_ref[...], weight_ref[...]))
    hidden = v_ref[:, CH:].astype(F32)
    cotangent = cot_ref[...].astype(F32)
    update = gates_ref[:, CH:]
    update_grad = cotangent * (hidden - candidate)
    grad = cotangent * (1.0 - update) * (1.0 - candidate * candidate)
    grads_ref[:, :CH] = grad.astype(BF)
    grads_ref[:, CH:] = (update_grad * update * (1.0 - update)).astype(BF)
    return_lists(*back_rims(grads_ref[:, :CH], turned_ref), out, inner_out)


def same_sample(products):
    low = lax.broadcasted_iota(jnp.int32, (HID, CH), 1) < HID
    top, bottom = products[:HID], products[HID:]
    return jnp.where(
        low,
        top[:, :CH] + pltpu.roll(bottom[:, :CH], HID, 1),
        pltpu.roll(top[:, CH:], HID, 1) + bottom[:, CH:],
    )


def totals_of(grad):
    products = t_mm(grad, jnp.ones((PAIR, 128), BF))
    return products[:HID] + products[HID:]


def gate_sums_of(grad, v_ref, hop_ref, second_ref, out_ref):
    products = [t_mm(grad, ref[...]) for ref in (v_ref, hop_ref, second_ref)]
    for k, (which, at) in enumerate(((0, 0), (1, 0), (2, 0), (1, SPAN), (2, SPAN))):
        out_ref[:, k * CH : (k + 1) * CH] = same_sample(products[which][:, at : at + SPAN])
    out_ref[:, KS * CH :] = totals_of(grad)


def candidate_sums_kernel(
    v_ref, hop_ref, second_ref, gated_ref, hidden_hop, hidden_second, grads_ref, sums_ref
):
    grad = grads_ref[:, :CH]
    supports = zip(
        supports_of(v_ref, hop_ref, second_ref, SPAN),
        supports_of(gated_ref, hidden_hop, hidden_second, CH),
    )
    for k, ((ref, at), (hidden_ref, hidden_at)) in enumerate(supports):
        products = jnp.concatenate(
            [
                t_mm(grad, ref[:, at : at + CH]),
                t_mm(grad, hidden_ref[:, hidden_at : hidden_at + CH]),
            ],
            1,
        )
        sums_ref[:HID, k * CH : (k + 1) * CH] = same_sample(products)
    sums_ref[:HID, KS * CH :] = totals_of(grad)
    gate_sums_of(grads_ref[:, CH:], v_ref, hop_ref, second_ref, sums_ref.at[HID:, :])


def back_hop(grad, width, turned_ref, pick_ref, to_a, to_b, weight_ref, base_ref):
    def product(left, k):
        return mm_t(left, weight_ref[ORDER[k] * SPAN : (ORDER[k] + 1) * SPAN, :])

    rim = []
    for part, coming in enumerate((to_a, to_b)):
        at = slice(part * PART, (part + 1) * PART)
        turned = turned_ref[part * EXT : (part + 1) * EXT, :]
        mine = grad[at]
        back = t_mm(pick_ref[part * HALO : (part + 1) * HALO, :], coming)
        pair = []
        for way in range(2):
            once = mm(turned[:PART, way * PART : (way + 1) * PART], mine)
            once = (2.0 * (once + back[:, way * width : (way + 1) * width])).astype(BF)
            pair.append((product(mine, 1 + 2 * way) + product(once, 2 + 2 * way)).astype(BF))
        spread = mm(turned, jnp.concatenate(pair, 0))
        rim.append(spread[PART:])
        base_ref[at, :] = (
            spread[:PART] + product(mine, 0) - product(mine, 2) - product(mine, 4)
        )
    return rim


def candidate_back_kernel(
    count, grads_ref, turned_ref, pick_ref, got, other, inner, weight_ref, early_ref,
    firsts_ref, out, inner_out,
):
    rim = []
    for part, coming in enumerate(arrivals(got, other, inner, count)):
        turned = turned_ref[part * EXT : (part + 1) * EXT, :]
        mine = grads_ref[part * PART : (part + 1) * PART, :CH]
        back = t_mm(pick_ref[part * HALO : (part + 1) * HALO, :], coming)
        for way in range(2):
            once = mm(turned[:PART, way * PART : (way + 1) * PART], mine)
            once = (2.0 * (once + back[:, way * CH : (way + 1) * CH])).astype(BF)
            at = (1 + 2 * way) * CH
            both = jnp.concatenate([mine, once], 1)
            row = part * PAIR + way * PART
            firsts_ref[row : row + PART, :] = mm(both, weight_ref[at : at + 2 * CH, :]).astype(BF)
        rim.append(mm(turned[PART:, :], firsts_ref[part * PAIR : (part + 1) * PAIR, :]))
    return_lists(rim[0], rim[1], out, inner_out)


def candidate_base_kernel(grads_ref, turned_ref, firsts_ref, weight_ref, base_ref):
    for part in range(2):
        at = slice(part * PART, (part + 1) * PART)
        mine = grads_ref[at, :CH]
        base_ref[at, :] = (
            mm(
                turned_ref[part * EXT : part * EXT + PART, :],
                firsts_ref[part * PAIR : (part + 1) * PAIR, :],
            )
            + mm(mine, weight_ref[0:CH, :])
            - mm(mine, weight_ref[2 * CH : 3 * CH, :])
            - mm(mine, weight_ref[4 * CH : 5 * CH, :])
        )


def arrivals_of_pairs(first, second, inner, count):
    got = jnp.where(core_id() == 0, first, second)
    other = jnp.where(core_id() == 0, second, first)
    return arrivals(got, other, inner, count)


def mixed_kernel(
    count, base_ref, got, other, inner, pick_ref, turned_ref, gates_ref, v_ref, grads_ref,
    early_ref, mixed_ref, gate_grads_ref, first_out, second_out, inner_out,
):
    for part, coming in enumerate(arrivals(got, other, inner, count)):
        at = slice(part * PART, (part + 1) * PART)
        mixed_ref[at, :] = base_ref[at, :] + t_mm(
            pick_ref[part * HALO : (part + 1) * HALO, :], coming
        )
    reset = gates_ref[:, :CH]
    grad = mixed_ref[:, CH:] * v_ref[:, CH:].astype(F32) * reset * (1.0 - reset)
    gate_grads_ref[:, :CH] = grad.astype(BF)
    gate_grads_ref[:, CH:] = grads_ref[:, CH:]
    return_both(
        *back_rims(gate_grads_ref[...], turned_ref), first_out, second_out, inner_out
    )


def folded(piece):
    return jnp.concatenate([piece[:, : WIDE // 2], piece[:, WIDE // 2 :]], 0)


def sums_kernel(
    quarters, size, v_ref, hop_ref, support_ref, gate_grads_ref, early_ref, first_ref, second_ref,
    own_ref, *rest
):
    outs, all_ref = rest[:-1], rest[-1]

    @pl.when(core_id() == 0)
    def _():
        for out, ref in zip(outs, (first_ref, second_ref)):
            out[0:96, :] = ref[...]

    @pl.when(core_id() == 1)
    def _():
        me = lax.axis_index("batch")
        all_ref[:HID, :] = early_ref[:HID, :]
        gate_sums_of(
            gate_grads_ref[:, :CH], v_ref, hop_ref, support_ref, all_ref.at[HID : 2 * HID, :]
        )
        all_ref[2 * HID :, :] = early_ref[HID:, :]
        own_ref[...] = folded(all_ref[rows_at(me, size), :])
        for step in range(1, quarters):
            piece = all_ref[rows_at(lax.rem(me + step, quarters), size), :]
            outs[step - 1][0 : 2 * size, 0 : WIDE // 2] = folded(piece).astype(BF)


def arrived_kernel(quarters, size, own_ref, *refs):
    got, out = refs[:-1], refs[-1]

    @pl.when(core_id() == 1)
    def _():
        total = own_ref[...]
        for ref in got[: quarters - 1]:
            total = total + ref[0 : 2 * size, 0 : WIDE // 2].astype(F32)
        out[0 : 2 * size, 0 : WIDE // 2] = total.astype(BF)


def gate_back_kernel(
    count, first_got, second_got, inner, grads_ref, turned_ref, pick_ref, weight_ref,
    first_out, second_out, inner_out, base_ref,
):
    @pl.when(core_id() == 0)
    def _():
        to_a, to_b = arrivals_of_pairs(first_got[0:96, :], second_got[0:96, :], inner, count)
        rim = back_hop(
            grads_ref[...], SPAN, turned_ref, pick_ref, to_a, to_b, weight_ref, base_ref
        )
        return_both(rim[0], rim[1], first_out, second_out, inner_out)


def turn_kernel_of(size, mine_ref, got_ref, list_ref, out):
    @pl.when(core_id() == 0)
    def _():
        out[0:96, 0:SPAN] = list_ref[...]

    @pl.when(core_id() == 1)
    def _():
        at = (slice(0, 2 * size), slice(0, WIDE // 2))
        out[at] = (mine_ref[at].astype(F32) + got_ref[at].astype(F32)).astype(BF)


def third_sum_kernel(size, mine_ref, got_ref, out):
    at = (slice(0, 2 * size), slice(0, WIDE // 2))
    out[...] = (mine_ref[at].astype(F32) + got_ref[at].astype(F32)).astype(out.dtype)


def last_kernel(
    count, first_got, second_got, base_ref, inner, pick_ref, mixed_ref, gates_ref, cot_ref,
    a_ref, b_ref,
):
    @pl.when(core_id() == 0)
    def _():
        coming = arrivals_of_pairs(
            first_got[0:96, 0:SPAN], second_got[0:96, 0:SPAN], inner, count
        )
        for part, out_ref in enumerate((a_ref, b_ref)):
            at = slice(part * PART, (part + 1) * PART)
            picks = pick_ref[part * HALO : (part + 1) * HALO, :]
            total = base_ref[at, :] + t_mm(picks, coming[part])
            mixed = mixed_ref[at, :]
            gates = gates_ref[at, :]
            out_ref[:, :CH] = mixed[:, :CH] + total[:, :CH]
            out_ref[:, CH:] = (
                cot_ref[at, :].astype(F32) * gates[:, CH:]
                + mixed[:, CH:] * gates[:, :CH]
                + total[:, CH:]
            )


def moved(value, place):
    width = lax.axis_size("batch")
    pairs = []
    for index in range(lax.axis_size("graph") * width):
        graph, y = divmod(index, width)
        chip, core, y = place(graph // 2, graph % 2, y)
        pairs.append((index, (2 * chip + core) * width + y))
    return lax.ppermute(value, ("graph", "batch"), pairs)


def turned_by(value, steps):
    width = lax.axis_size("batch")
    return moved(value, lambda chip, core, y: (chip, core, (y + steps) % width))


def swapped(value):
    return moved(value, lambda chip, core, y: (chip, 1 - core, y))


def paired(value, partners):
    return moved(value, lambda chip, core, y: (partners[chip], core, y))


def to_neighbours(chip, core, y):
    count = lax.axis_size("graph") // 2
    if core == 0:
        return chip ^ 1, core, y
    other = chip + 1 - 2 * ((chip + 1) % 2)
    if 0 <= other < count:
        return other, core, y
    return (chip, core, y ^ 1) if lax.axis_size("batch") % 2 == 0 else (other % count, core, y)


def exchange(out, beside=()):
    got = moved(out, to_neighbours)
    if beside:
        got = summed([got], got.dtype, "relay", after=beside)[0]
    return got, swapped(got)


def to_first(chip, y):
    return chip ^ 1, y


def to_second(chip, y):
    chip, _, y = to_neighbours(chip, 1, y)
    return chip, y


def by_core(value, first_place, second_place):
    def place(chip, core, y):
        to_chip, to_y = (second_place if core else first_place)(chip, y)
        return to_chip, core, to_y

    return moved(value, place)


def round_batch(steps):
    width = lax.axis_size("batch")
    return lambda chip, y: (chip, (y + steps) % width)


def to_partner(partners):
    return lambda chip, y: (partners[chip], y)


def ring_steps(length):
    if length == 8:
        return [[i ^ 1 for i in range(8)], [i ^ 2 for i in range(8)], [6, 7, 4, 5, 2, 3, 0, 1]]
    if length == 4:
        return [[1, 0, 3, 2], [3, 2, 1, 0]]
    return [[1, 0]] if length == 2 else []


def chip_steps(chips):
    ring = math.gcd(chips, 8)
    inside = [
        [chip - chip % ring + step[chip % ring] for chip in range(chips)]
        for step in ring_steps(ring)
    ]
    between = [
        [step[chip // ring] * ring + chip % ring for chip in range(chips)]
        for step in ring_steps(chips // ring)
    ]
    return inside, between


def sum_kernel(terms, count, *refs):
    total = refs[0][...].astype(F32)
    for ref in refs[1:terms]:
        total = total + ref[...].astype(F32)
    outs = refs[count:]
    outs[0][...] = total.astype(outs[0].dtype)
    for out, ref in zip(outs[1:], refs[terms:]):
        out[...] = ref[...]


def summed(terms, dtype, name, after=(), through=()):
    args = list(terms) + list(through) + list(after)
    return call(
        lambda *refs: sum_kernel(len(terms), len(args), *refs),
        [(terms[0].shape, dtype)] + [(array.shape, array.dtype) for array in through],
        args,
        name,
    )


def gathered_kernel(quarters, size, *refs):
    me = lax.axis_index("batch")
    for step in range(quarters):
        source = lax.rem(me - step + quarters, quarters)
        piece = refs[step]
        refs[-1][rows_at(source, size), :] = jnp.concatenate([piece[:size], piece[size:]], 1)


def scaled_kernel(
    scale, mine_ref, got_ref, own_result, got_result,
    input_ref, state_ref, gate_ref, gate_bias_ref, candidate_ref, candidate_bias_ref,
):
    result = jnp.where(core_id() == 0, own_result[...], got_result[...])
    input_ref[...] = result[:, :CH]
    state_ref[...] = result[:, CH:]
    total = jnp.where(core_id() == 1, mine_ref[...], got_ref[...]).astype(F32) * scale
    candidate_ref[...] = total[:HID, : KS * CH]
    for k in range(KS):
        at = slice(k * CH, (k + 1) * CH)
        gate_ref[at, :] = total[HID:, at].T
    candidate_bias_ref[...] = total[:HID, KS * CH :].T[:1]
    gate_bias_ref[...] = total[HID:, KS * CH :].T[:1]


def on_device(
    layer_input,
    hidden_state,
    hidden_grad,
    gate_weight,
    gate_bias,
    candidate_weight,
    candidate_bias,
    forward_tiles,
    forward_columns,
    reverse_tiles,
    reverse_columns,
    send_rows,
    send_count,
):
    count = lax.axis_size("graph") // 2

    def with_count(body):
        return lambda *refs: body(count, *refs)

    own = call(
        load_kernel,
        [((PART, 4 * CH), BF)],
        [
            layer_input, hidden_state, hidden_grad, send_rows, send_count, forward_columns,
            reverse_columns,
        ],
        "load",
        scratch=[
            pltpu.VMEM(array.shape, jnp.int32)
            for array in (send_rows, send_count, forward_columns, reverse_columns)
        ]
        + [pltpu.SemaphoreType.DMA((7,))],
        space=pltpu.HBM,
        limit=60 << 20,
    )[0]
    own_got = swapped(own)
    forward_got = swapped(forward_tiles)
    reverse_got = swapped(reverse_tiles)

    def lists(width):
        return [((96, width), BF), ((64, width), BF)]

    values, cotangent, picks, out, inner = call(
        start_kernel,
        [((PAIR, SPAN), BF), ((PAIR, CH), BF), ((2 * HALO, PART), BF)] + lists(SPAN),
        [own, own_got],
        "start",
    )
    maps = call(
        map_kernel,
        [((2 * PAIR, EXT), BF)],
        [forward_tiles, reverse_tiles, forward_got, reverse_got, own, own_got],
        "maps",
    )[0]
    gate_blocks, candidate_blocks, gate_biases, candidate_biases, blocks_turned, two_hop_blocks = call(
        weight_kernel,
        [
            ((KS * SPAN, SPAN), BF), ((KS * SPAN, CH), BF), ((8, SPAN), F32), ((8, CH), F32),
            ((KS * CH, SPAN), BF), ((SPAN, CH), BF),
        ],
        [gate_weight, candidate_weight.T, gate_bias[None, :], candidate_bias[None, :]],
        "weights",
    )
    got, other = exchange(out, [maps, gate_biases])
    hop, out, inner = call(
        with_count(gate_hop_kernel),
        [((PAIR, 2 * SPAN), BF)] + lists(2 * SPAN),
        [values, maps, picks, got, other, inner],
        "gate_hop",
    )
    got, other = exchange(out)
    gate_start = call(
        gate_start_kernel, [((PAIR, SPAN), F32)], [values, hop, gate_blocks, gate_biases],
        "gate_start",
    )[0]
    gate_hop = hop
    gate_second, gates, gated, out, inner = call(
        with_count(gate_kernel),
        [((PAIR, 2 * SPAN), BF), ((PAIR, SPAN), F32), ((PAIR, CH), BF)] + lists(CH),
        [values, hop, maps, picks, got, other, inner, gate_blocks, gate_start],
        "gates",
    )
    got, other = exchange(out)
    turned = call(turn_kernel, [((2 * EXT, PAIR), BF)], [maps], "turn")[0]
    hop, out, inner = call(
        with_count(candidate_hop_kernel),
        [((PAIR, SPAN), BF)] + lists(SPAN),
        [gated, maps, picks, got, other, inner, turned],
        "candidate_hop",
    )
    got, other = exchange(out)
    candidate_start = call(
        candidate_start_kernel,
        [((PAIR, CH), F32)],
        [values, gate_hop, gate_second, gated, hop, candidate_blocks, candidate_biases],
        "candidate_start",
    )[0]
    second_hops, grads, out, inner = call(
        with_count(candidate_kernel),
        [((PAIR, SPAN), BF), ((PAIR, SPAN), BF)] + lists(SPAN),
        [
            values, gated, hop, maps, turned, got, other, inner, gates, cotangent, candidate_start,
            two_hop_blocks,
        ],
        "candidate",
    )
    got, other = exchange(out)
    early = call(
        candidate_sums_kernel,
        [((CH, WIDE), F32)],
        [values, gate_hop, gate_second, gated, hop, second_hops, grads],
        "candidate_sums",
    )[0]
    firsts, out, inner = call(
        with_count(candidate_back_kernel),
        [((2 * PAIR, SPAN), BF)] + lists(SPAN),
        [grads, turned, picks, got, other, inner, blocks_turned, early],
        "candidate_back",
    )
    got, other = exchange(out)
    base = call(
        candidate_base_kernel,
        [((PAIR, SPAN), F32)],
        [grads, turned, firsts, blocks_turned],
        "candidate_base",
    )[0]
    mixed, gate_grads, first, second, inner = call(
        with_count(mixed_kernel),
        [((PAIR, SPAN), F32), ((PAIR, SPAN), BF), ((96, 2 * SPAN), BF)] + lists(2 * SPAN),
        [base, got, other, inner, picks, turned, gates, values, grads, early],
        "mixed",
    )
    quarters = lax.axis_size("batch")
    size = 3 * HID // quarters
    folds = (2 * size, WIDE // 2)
    shared = (max(96, folds[0]), 2 * SPAN)
    swaps = max(quarters - 1, 2)
    own, *pieces = call(
        lambda *refs: sums_kernel(quarters, size, *refs),
        [(folds, F32)] + [(shared, BF)] * 2 + [(folds, BF)] * (swaps - 2),
        [values, gate_hop, gate_second, gate_grads, early, first, second],
        "sums",
        scratch=[pltpu.VMEM((3 * HID, WIDE), F32)],
    )
    ways = [to_first, to_second] + [to_first] * (swaps - 2)
    arrived = {
        k: by_core(pieces[k], ways[k], round_batch(k + 1) if k + 1 < quarters else to_first)
        for k in [1, 0] + list(range(2, swaps))
    }
    arrived = [arrived[k] for k in range(swaps)]
    inside, between = chip_steps(count)
    steps = inside + between
    shared = (max(96, folds[0]), WIDE // 2)
    mine = call(
        lambda *refs: arrived_kernel(quarters, size, *refs), [(shared, BF)], [own] + arrived,
        "arrived",
    )[0]
    got = by_core(mine, to_first, to_partner(steps[0]))
    first, second, inner, base = call(
        with_count(gate_back_kernel),
        [((96, SPAN), BF), ((96, SPAN), BF), ((64, SPAN), BF), ((PAIR, SPAN), F32)],
        arrived[:2] + [inner, gate_grads, turned, picks, gate_blocks],
        "gate_back",
    )

    def turn(mine, got, listed):
        return call(
            lambda *refs: turn_kernel_of(size, *refs), [(shared, BF)], [mine, got, listed], "turn_in"
        )[0]

    mine = turn(mine, got, first)
    first_got = by_core(mine, to_first, to_partner(steps[1]))
    mine = turn(mine, first_got, second)
    third = to_partner(steps[2]) if len(steps) > 2 else lambda chip, y: (chip ^ 1, y)
    second_got = by_core(mine, to_second, third)
    if len(steps) > 2:
        mine = call(
            lambda *refs: third_sum_kernel(size, *refs), [(folds, BF)], [mine, second_got], "third"
        )[0]
    else:
        mine = mine[: folds[0], : folds[1]].astype(F32)
    for_first, for_second = call(
        with_count(last_kernel),
        [((PART, SPAN), F32), ((PART, SPAN), F32)],
        [first_got, second_got, base, inner, picks, mixed, gates, cotangent],
        "last",
    )
    result_got = swapped(for_second)
    for number, partners in enumerate(steps[3:]):
        kind = F32 if number + 4 < len(steps) else BF
        got = by_core(mine, to_first, to_partner(partners))
        after = [result_got] if number == 1 else []
        mine = summed([mine, got], kind, "pair_sum", after=after)[0]
    mine = mine.astype(BF)
    around = {
        step: by_core(mine, to_first, round_batch(step)) if step else mine
        for step in sorted(range(quarters), key=lambda step: step != 2)
    }
    around = [around[step] for step in range(quarters)]
    mine = call(
        lambda *refs: gathered_kernel(quarters, size, *refs),
        [((3 * HID, WIDE), BF)],
        around,
        "gathered",
    )[0]
    samples = layer_input.shape[1] // HID * quarters
    scale = 1.0 / math.sqrt(PART * lax.axis_size("graph") * samples)
    input_total, hidden_total, gate_sums, gate_totals, candidate_sums, candidate_totals = call(
        lambda *refs: scaled_kernel(scale, *refs),
        [
            ((PART, CH), F32), ((PART, CH), F32), ((KS * CH, CH), F32), ((1, CH), F32),
            ((HID, KS * CH), F32), ((1, HID), F32),
        ],
        [mine, swapped(mine), for_first, result_got],
        "scaled",
    )
    return (
        input_total, hidden_total, gate_sums, gate_totals.reshape(-1), candidate_sums.T,
        candidate_totals.reshape(-1),
    )


def solution(mesh):
    placed = (
        P("graph", "batch"),
        P("graph", "batch"),
        P("graph", "batch"),
        P(),
        P(),
        P(),
        P(),
        P("graph", None, None, None),
        P("graph", None),
        P("graph", None, None, None),
        P("graph", None),
        P("graph", None, None),
        P("graph", None),
    )
    return jax.shard_map(
        on_device,
        mesh=mesh,
        in_specs=placed,
        out_specs=(P("graph", "batch"), P("graph", "batch"), P(), P(), P(), P()),
        check_vma=False,
    )
```
